256 devices in a mesh: section: 2 (over z_hi), dp: 8 (over z_lo, core), mp: 16 (over x, y).
Axes of the slice: x: 4, y: 4, z: 8 (z_hi: 2, z_lo: 4; z = z_hi * 4 + z_lo), core: 2. Of those that a mesh axis runs over, the one named last changes fastest.
Arguments:
- queries: bfloat16 [64, 4, 8192], P('dp'), may hold values from -48 to 48
- new_keys: bfloat16 [64, 4, 1024], P('dp'), may hold values from -6 to 6
- new_values: bfloat16 [64, 4, 1024], P('dp'), may hold values from -6 to 6
- cache_keys: bfloat16 [64, 512, 1024], P('dp', 'mp'), may hold values from -32 to 32
- cache_values: bfloat16 [64, 512, 1024], P('dp', 'mp'), may hold values from -6 to 6
- lengths: int32 [64], P('dp'), may hold values from 2 to 512, as said below
- out_weight: bfloat16 [8192, 8192], P('mp', ('section', 'dp')), may hold values from -0.0625 to 0.0625
- resid_expert: bfloat16 [256, 8192], P(None, ('section', 'dp')), may hold values from -8 to 8
- gain_expert: bfloat16 [8192], P(('section', 'dp')), may hold values from 0.25 to 1.75
- hidden_amateur: bfloat16 [256, 4096], P(None, ('section', 'dp')), may hold values from -8 to 8
- gain_amateur: bfloat16 [4096], P(('section', 'dp')), may hold values from 0.25 to 1.75
- head_expert: bfloat16 [131072, 8192], P(('section', 'dp', 'mp')), may hold values from -0.34250485 to 0.34250485
- head_amateur: bfloat16 [131072, 4096], P(('section', 'dp', 'mp')), may hold values from -0.484375 to 0.484375
- chosen: int32 [64, 4], replicated, may hold values from 0 to 131071
Outputs:
- scores: bfloat16 [64, 4, 131072], P(None, None, ('section', 'dp', 'mp'))
- chosen_score: float32 [64, 4], replicated
The draws below stay inside these ranges and needn't reach their ends.
Inputs may be any that keep to these rules, and one draw needn't show every extreme that they name: `lengths`: some sequence has 512 cached positions.
All inputs are finite; a program needn't handle non-finite values.
Results may differ from the reference program's by a relative error of at most 0.0034.
Values may be sent and summed in bfloat16 or wider, within the bound.
A program may use at most 128 MiB of HBM per device.

```python
import math
import jax
import jax.numpy as jnp
from jax import lax

DE = 8192
DA = 4096
HEADS = 64
KVH = 8
HD = 128
STEPS = 4
ROWS = 64
TOKENS = 256
CTX = 512
VOCAB = 131072


def attention_pairs(key):
    key_rows = jax.random.fold_in(key, 0)
    key_heads = jax.random.fold_in(key, 2)
    key_base = jax.random.fold_in(key, 3)
    row_pick = jax.random.permutation(key_rows, ROWS)[:3]
    head_pick = jax.random.randint(key_heads, (3,), 0, HEADS)
    base_vectors = 3.0 * jax.random.normal(key_base, (3, HD), jnp.float32)
    return (row_pick, head_pick, base_vectors)


def vocab_pairs(key, salt, width):
    key_local = jax.random.fold_in(key, salt)
    key_ids = jax.random.fold_in(key_local, 1)
    key_base = jax.random.fold_in(key_local, 2)
    id_pick = jax.random.permutation(key_ids, VOCAB)[:6]
    base_vectors = jnp.clip(jax.random.normal(key_base, (3, width), jnp.float32), -5.0, 5.0)
    return (id_pick, base_vectors)


def draw_queries(key, part):
    key = jax.random.fold_in(key, 1)
    table = jax.random.normal(key, (ROWS, STEPS, HEADS, HD), jnp.float32)
    return table.reshape(ROWS, STEPS, HEADS * HD).astype(jnp.bfloat16)


def draw_cache_keys(key, part):
    row_pick, head_pick, base_vectors = attention_pairs(key)
    key = jax.random.fold_in(key, 2)
    key_scale, key_entry = jax.random.split(key)
    scales = jnp.exp(jax.random.uniform(key_scale, (ROWS, CTX, KVH, 1), jnp.float32, math.log(0.3), math.log(3.0)))
    entry = jax.random.normal(key_entry, (ROWS, CTX, KVH, HD), jnp.float32)
    table = entry * scales
    kv_pick = head_pick // (HEADS // KVH)
    table = table.at[row_pick, 0, kv_pick].set(base_vectors)
    table = table.at[row_pick, 1, kv_pick].set(0.99 * base_vectors)
    return table.reshape(ROWS, CTX, KVH * HD).astype(jnp.bfloat16)


def draw_lengths(key, part):
    key = jax.random.fold_in(key, 3)
    key_lens, key_top = jax.random.split(key)
    counts = jax.random.randint(key_lens, (ROWS,), 2, CTX + 1)
    longest = jax.random.randint(key_top, (), 0, ROWS)
    return counts.at[longest].set(CTX)


def residual_table(key, salt, width):
    key = jax.random.fold_in(key, salt + 100)
    table = jax.random.normal(key, (TOKENS, width), jnp.float32)
    return table


def head_table(key, salt, width, entry):
    id_pick, base_vectors = vocab_pairs(key, salt, width)
    key_scale = jax.random.fold_in(key, salt + 200)
    scales = jnp.exp(jax.random.uniform(key_scale, (VOCAB, 1), jnp.float32, math.log(0.6), math.log(6.0))) / math.sqrt(width)
    table = jnp.clip(entry, -5.0, 5.0) * scales
    strengths = jnp.array([3.8, 3.2, 2.8], jnp.float32)
    aligned = strengths[:, None] * base_vectors / math.sqrt(width)
    table = table.at[id_pick[:3]].set(aligned)
    table = table.at[id_pick[3:]].set(aligned * (1.0 - 2.0 / (strengths[:, None] * math.sqrt(width))))
    return table


def draw_resid_expert(key, part):
    return residual_table(key, 7, DE).astype(jnp.bfloat16)


def draw_hidden_amateur(key, part):
    return residual_table(key, 9, DA).astype(jnp.bfloat16)


def draw_head_expert(key, part):
    key_entry = jax.random.fold_in(key, 4)
    entry = jax.random.normal(key_entry, (VOCAB, DE), jnp.float32)
    return head_table(key, 7, DE, entry).astype(jnp.bfloat16)


def draw_head_amateur(key, part):
    key_entry = jax.random.fold_in(key, 5)
    entry = jax.random.normal(key_entry, (VOCAB, DA), jnp.float32)
    return head_table(key, 9, DA, entry).astype(jnp.bfloat16)


def set_ends(drawn, rng, least, largest):
    shape = drawn.shape
    index_at = [jax.random.randint(jax.random.fold_in(rng, axis), (), 0, shape[axis]) for axis in range(len(shape))]
    drawn = drawn.at[tuple(index_at)].set(least)
    longest = shape.index(max(shape))
    index_at[longest] = (index_at[longest] + 1) % shape[longest]
    return drawn.at[tuple(index_at)].set(largest)


def block_scale(own_key, extent, cuts, smallest, largest):
    loudness = 1.0
    for dim, blocks in cuts:
        steps = jax.random.uniform(jax.random.fold_in(jax.random.fold_in(own_key, 6), dim), (blocks,), jnp.float32, smallest / len(cuts), largest / len(cuts))
        loudness = loudness * jnp.repeat(jnp.exp(steps), extent[dim] // blocks).reshape((-1,) + (1,) * (len(extent) - 1 - dim))
    return loudness


def bell_draw(stream_key, dims, deviation, most, pieces=(), kind=jnp.bfloat16):
    values = jax.random.normal(stream_key, dims, jnp.float32) * deviation
    if len(pieces) > 0:
        values = block_scale(stream_key, dims, pieces, -0.22, 0.18) * values
    return jnp.clip(values, min=-most, max=most).astype(kind)


def setup_inputs(seed: int = 0) -> dict:
    arg_keys = jax.random.split(jax.random.key(seed), 15)
    queries = draw_queries(jax.random.fold_in(arg_keys[14], 71), 0)
    new_keys = bell_draw(arg_keys[1], (ROWS, STEPS, KVH * HD), 1.0, 6.0, ((0, 8),))
    new_values = bell_draw(arg_keys[2], (ROWS, STEPS, KVH * HD), 1.0, 6.0, ((0, 8),))
    cache_keys = draw_cache_keys(jax.random.fold_in(arg_keys[14], 71), 0)
    cache_values = bell_draw(arg_keys[4], (ROWS, CTX, KVH * HD), 1.0, 6.0, ((0, 8), (1, 16)))
    lengths = draw_lengths(jax.random.fold_in(arg_keys[14], 71), 0)
    out_weight = bell_draw(arg_keys[6], (HEADS * HD, DE), (HEADS * HD) ** -0.5, 0.0625, ((0, 16), (1, 16)))
    resid_expert = draw_resid_expert(jax.random.fold_in(arg_keys[14], 71), 0)
    gain_expert = jnp.clip(1.0 + 0.15 * jax.random.normal(arg_keys[8], (DE,), jnp.float32), 0.25, 1.75).astype(jnp.bfloat16)
    hidden_amateur = draw_hidden_amateur(jax.random.fold_in(arg_keys[14], 71), 0)
    gain_amateur = jnp.clip(1.0 + 0.15 * jax.random.normal(arg_keys[10], (DA,), jnp.float32), 0.25, 1.75).astype(jnp.bfloat16)
    head_expert = draw_head_expert(jax.random.fold_in(arg_keys[14], 71), 0)
    head_amateur = draw_head_amateur(jax.random.fold_in(arg_keys[14], 71), 0)
    chosen = set_ends(jax.random.randint(arg_keys[13], (ROWS, STEPS), 0, VOCAB), jax.random.fold_in(arg_keys[13], 1), 0, VOCAB - 1).astype(jnp.int32)
    return {"queries": queries, "new_keys": new_keys, "new_values": new_values, "cache_keys": cache_keys, "cache_values": cache_values, "lengths": lengths, "out_weight": out_weight, "resid_expert": resid_expert, "gain_expert": gain_expert, "hidden_amateur": hidden_amateur, "gain_amateur": gain_amateur, "head_expert": head_expert, "head_amateur": head_amateur, "chosen": chosen}


CONTRAST = 0.5
NEGATIVE = -1e+30
EPSILON = 1e-05

def normalize(hidden, gain_vector):
    widened = hidden.astype(jnp.float32)
    mean_sq = lax.optimization_barrier(jnp.mean(widened * widened, axis=1, keepdims=True))
    return (widened * lax.rsqrt(mean_sq + EPSILON) * gain_vector.astype(jnp.float32)).astype(jnp.bfloat16)

def partial_attention(queries, new_keys, new_values, cache_keys, cache_values, lengths, offset, with_new):
    row_count = queries.shape[0]
    step_count = queries.shape[1]
    span_len = cache_keys.shape[1]
    group_size = queries.shape[2] // (KVH * HD)
    query_all = queries.reshape(row_count, step_count, KVH, group_size, HD)
    keys_old = cache_keys.reshape(row_count, span_len, KVH, HD)
    values_old = cache_values.astype(jnp.float32).reshape(row_count, span_len, KVH, HD)
    keys_new = new_keys.reshape(row_count, step_count, KVH, HD)
    values_new = new_values.astype(jnp.float32).reshape(row_count, step_count, KVH, HD)
    scaling = 1.0 / HD ** 0.5
    scores_old = jnp.einsum('rsghd,rpgd->rsghp', query_all, keys_old, preferred_element_type=jnp.float32) * scaling
    scores_new = jnp.einsum('rsghd,rtgd->rsght', query_all, keys_new, preferred_element_type=jnp.float32) * scaling
    positions = offset + jnp.arange(span_len, dtype=jnp.int32)
    live_old = (positions[None, :] < lengths[:, None])[:, None, None, None, :]
    step_order = jnp.arange(step_count, dtype=jnp.int32)
    live_new = ((step_order[None, :] <= step_order[:, None]) & with_new)[None, :, None, None, :]
    scores_old = jnp.where(live_old, scores_old, NEGATIVE)
    scores_new = jnp.where(live_new, scores_new, NEGATIVE)
    column_max = jnp.maximum(lax.optimization_barrier(jnp.max(scores_old, axis=-1)), lax.optimization_barrier(jnp.max(scores_new, axis=-1)))
    weights_old = jnp.where(live_old, jnp.exp(scores_old - column_max[..., None]), 0.0)
    weights_new = jnp.where(live_new, jnp.exp(scores_new - column_max[..., None]), 0.0)
    totals = lax.optimization_barrier(jnp.sum(weights_old, axis=-1)) + lax.optimization_barrier(jnp.sum(weights_new, axis=-1))
    mixture = jnp.einsum('rsghp,rpgd->rsghd', weights_old, values_old, precision=lax.Precision.HIGHEST)
    mixture = mixture + jnp.einsum('rsght,rtgd->rsghd', weights_new, values_new, precision=lax.Precision.HIGHEST)
    head_count = KVH * group_size
    return (column_max.reshape(row_count, step_count, head_count), totals.reshape(row_count, step_count, head_count), mixture.reshape(row_count, step_count, head_count, HD))

def log_total(logits):
    top_value = lax.optimization_barrier(jnp.max(logits, axis=1))
    return top_value + jnp.log(lax.optimization_barrier(jnp.sum(jnp.exp(logits - top_value[:, None]), axis=1)))

def reference(queries, new_keys, new_values, cache_keys, cache_values, lengths, out_weight, resid_expert, gain_expert, hidden_amateur, gain_amateur, head_expert, head_amateur, chosen):
    column_max, totals, mixture = partial_attention(queries, new_keys, new_values, cache_keys, cache_values, lengths, 0, True)
    attended = (mixture / totals[..., None]).astype(jnp.bfloat16).reshape(TOKENS, HEADS * HD)
    projected = jnp.dot(attended, out_weight, preferred_element_type=jnp.float32)
    hidden_expert = (resid_expert.astype(jnp.float32) + projected).astype(jnp.bfloat16)
    normed_expert = normalize(hidden_expert, gain_expert)
    normed_amateur = normalize(hidden_amateur, gain_amateur)
    logits_expert = lax.dot_general(normed_expert, head_expert, (((1,), (1,)), ((), ())), preferred_element_type=jnp.float32)
    logits_amateur = lax.dot_general(normed_amateur, head_amateur, (((1,), (1,)), ((), ())), preferred_element_type=jnp.float32)
    lse_expert = log_total(logits_expert)
    lse_amateur = log_total(logits_amateur)
    contrast_all = logits_expert - lse_expert[:, None] - CONTRAST * (logits_amateur - lse_amateur[:, None])
    scores = contrast_all.astype(jnp.bfloat16).reshape(ROWS, STEPS, VOCAB)
    chosen_score = jnp.take_along_axis(contrast_all, chosen.reshape(TOKENS, 1).astype(jnp.int32), axis=1).reshape(ROWS, STEPS)
    return (scores, chosen_score)
```

```python
import jax
import jax.numpy as jnp
from jax import lax
from jax.experimental import pallas as pl
from jax.experimental.pallas import tpu as pltpu
from jax.sharding import PartitionSpec as P

MESH = pl.DeviceIdType.MESH
F32 = jnp.float32
BF16 = jnp.bfloat16
KVH = 8
HD = 128
CONTRAST = 0.5
NEGATIVE = -1e30
EPSILON = 1e-05
NT = (((1,), (1,)), ((), ()))
TN = (((0,), (0,)), ((), ()))


def rcopy(src, dst, send_sem, recv_sem, device):
    return pltpu.make_async_remote_copy(
        src_ref=src,
        dst_ref=dst,
        send_sem=send_sem,
        recv_sem=recv_sem,
        device_id=device,
        device_id_type=MESH,
    )


def iota(shape, dim):
    return lax.broadcasted_iota(jnp.int32, shape, dim)


def kernel(
    lengths,
    queries,
    new_keys,
    new_values,
    resid,
    gain_expert,
    gain_amateur,
    hidden_amateur,
    chosen,
    cache_keys,
    cache_values,
    out_weight,
    head_expert,
    head_amateur,
    out,
    out_chosen,
    keys_v,
    values_v,
    weight_v,
    he_v,
    ha_v,
    state_out,
    state_in,
    scale_t,
    attended,
    part_out,
    part_in,
    full,
    amateur,
    acc_e,
    acc_a,
    square_e,
    square_a,
    diff,
    stats_p,
    stats_z,
    load_sem,
    state_sem,
    attended_sem,
    part_sem,
    one_sem,
    two_sem,
    three_send,
    three_recv,
    relay_send,
    relay_recv,
    am_send,
    am_recv,
    am_rsend,
    am_rrecv,
    stats_sem,
):
    sec = lax.axis_index("section")
    dp = lax.axis_index("dp")
    mp = lax.axis_index("mp")
    z = sec * 4 + dp // 2
    c = dp % 2
    n = sec * 8 + dp
    x, y = mp // 4, mp % 4
    u = x * (1 - c) + y * c
    v = y * (1 - c) + x * c

    def at_n(k):
        return (k // 8, k % 8, mp)

    def at_z(zz):
        return (zz // 4, (zz % 4) * 2 + c, mp)

    def at_mp(k):
        return (sec, dp, k)

    def at_uv(uu, vv):
        return (sec, dp, (uu * 4 + vv) * (1 - c) + (vv * 4 + uu) * c)

    sibling = (sec, dp + 1 - 2 * c, mp)

    loads = [
        pltpu.make_async_copy(cache_keys.at[pl.ds(sec * 4, 4)], keys_v, load_sem.at[0]),
        pltpu.make_async_copy(cache_values.at[pl.ds(sec * 4, 4)], values_v, load_sem.at[1]),
        pltpu.make_async_copy(out_weight, weight_v, load_sem.at[2]),
        pltpu.make_async_copy(head_amateur, ha_v, load_sem.at[3]),
        pltpu.make_async_copy(head_expert, he_v, load_sem.at[4]),
    ]

    barrier = pltpu.get_barrier_semaphore()

    def greet(k, carry):
        pl.semaphore_signal(
            barrier, inc=1, device_id=at_mp((mp + k) % 16), device_id_type=MESH
        )
        pl.semaphore_signal(
            barrier, inc=1, device_id=at_n((n + k) % 16), device_id_type=MESH
        )
        return carry

    lax.fori_loop(1, 16, greet, 0)
    for load in loads:
        load.start()

    amateur[c, z, 0:256, :] = hidden_amateur[...]
    row16 = iota((16, 256), 0)
    gains = jnp.where(
        row16 == 0,
        gain_expert[:, 0:256].astype(F32),
        jnp.where(
            row16 == 1,
            gain_expert[:, 256:512].astype(F32),
            jnp.where(row16 == 2, gain_amateur[...].astype(F32), 0.0),
        ),
    )
    amateur[c, z, 256:272, :] = gains.astype(BF16)
    pl.semaphore_wait(barrier, 30)

    def am_copy(way, step):
        if way == 0:
            block, target = (z - step + 9) % 8, (z + 1) % 8
        else:
            block, target = (z + step - 1) % 8, (z + 7) % 8
        ref = amateur.at[c, block]
        return rcopy(ref, ref, am_send.at[way, step], am_recv.at[way, step], at_z(target))

    def am_relay(block):
        ref = amateur.at[c, block]
        return rcopy(ref, ref, am_rsend.at[block], am_rrecv.at[block], sibling)

    def am_advance(step):
        am_copy(0, step).wait_recv()
        if step < 4:
            am_copy(0, step + 1).start()
        am_relay((z - step + 8) % 8).start()
        if step < 4:
            am_copy(1, step).wait_recv()
            if step < 3:
                am_copy(1, step + 1).start()
            am_relay((z + step) % 8).start()

    am_copy(0, 1).start()
    am_copy(1, 1).start()
    am_relay(z).start()

    row_i, col_i = iota((128, 128), 0), iota((128, 128), 1)
    limit = jnp.zeros((128, 128), jnp.int32)
    for r in range(4):
        limit = jnp.where(row_i // 32 == r, lengths[sec * 4 + r], limit)
    live_old = (row_i // 32 == (col_i // 4) % 4) & (row_i % 32 + mp * 32 < limit)
    row_n, col_n = iota((16, 128), 0), iota((16, 128), 1)
    live_new = (row_n // 4 == (col_n // 4) % 4) & (row_n % 4 <= col_n % 4) & (mp == 0)
    loads[0].wait()
    loads[1].wait()

    def stacked(ref, start):
        part = ref[pl.ds(sec * 4, 4), :, pl.ds(start, HD)].astype(F32)
        return jnp.concatenate([part[r] for r in range(4)], axis=0)

    def attend(i, carry):
        g = (mp // 2 + 1 + i) % 8
        base = pl.multiple_of(g * HD, HD)
        keys_old = keys_v[:, :, pl.ds(base, HD)].reshape(128, HD)
        values_old = values_v[:, :, pl.ds(base, HD)].reshape(128, HD)
        keys_new = stacked(new_keys, base).astype(BF16)
        values_new = stacked(new_values, base).astype(BF16)
        query = jnp.concatenate(
            [stacked(queries, pl.multiple_of(g * 1024 + h * HD, HD)) for h in range(8)], axis=0
        ).astype(BF16)
        scaling = 1.0 / HD**0.5
        s_old = lax.dot_general(keys_old, query, NT, preferred_element_type=F32) * scaling
        s_new = lax.dot_general(keys_new, query, NT, preferred_element_type=F32) * scaling
        s_old = jnp.where(live_old, s_old, NEGATIVE)
        s_new = jnp.where(live_new, s_new, NEGATIVE)
        top = jnp.maximum(
            jnp.max(s_old, axis=0, keepdims=True), jnp.max(s_new, axis=0, keepdims=True)
        )
        top = top.astype(BF16).astype(F32)
        p_old = jnp.where(live_old, jnp.exp(s_old - top), 0.0)
        p_new = jnp.where(live_new, jnp.exp(s_new - top), 0.0)
        total = jnp.sum(p_old, axis=0, keepdims=True) + jnp.sum(p_new, axis=0, keepdims=True)
        mix = lax.dot_general(
            p_old.astype(BF16), values_old, TN, preferred_element_type=F32
        ) + lax.dot_general(p_new.astype(BF16), values_new, TN, preferred_element_type=F32)
        high = total.astype(BF16).astype(F32)
        tile = jnp.where(
            row_n == 0,
            top,
            jnp.where(row_n == 1, high, jnp.where(row_n == 2, total - high, 0.0)),
        ).astype(BF16)
        mix = mix.astype(BF16)
        for e in range(2):
            dest = 2 * g + e
            state_out[dest, 0:64, :] = mix[e * 64 : e * 64 + 64]
            state_out[dest, 64:80, :] = tile

            @pl.when(dest != mp)
            def _():
                rcopy(
                    state_out.at[dest],
                    state_in.at[mp],
                    state_sem.at[0],
                    state_sem.at[1],
                    at_mp(dest),
                ).start()

        return carry

    lax.fori_loop(0, 8, attend, 0)
    state_in[mp] = state_out[mp]
    am_advance(1)
    fifteen = pl.ds(0, 15)
    state_all = rcopy(
        state_out.at[fifteen], state_in.at[fifteen], state_sem.at[0], state_sem.at[1], sibling
    )
    state_all.wait_recv()

    tiles = [state_in[k, 64:80, :].astype(F32) for k in range(16)]
    top = tiles[0][0:1]
    for k in range(1, 16):
        top = jnp.maximum(top, tiles[k][0:1])
    total = jnp.zeros((1, 128), F32)
    weights = jnp.zeros((128, 128), F32)
    for k in range(16):
        scale = jnp.exp(tiles[k][0:1] - top)
        total = total + scale * (tiles[k][1:2] + tiles[k][2:3])
        weights = jnp.where(row_i == k, scale, weights)
    scale_t[...] = (weights / total).T
    own = scale_t[pl.ds(pl.multiple_of((mp % 2) * 64, 64), 64), :]
    mixed = jnp.zeros((64, HD), F32)
    for k in range(16):
        mixed = mixed + own[:, k : k + 1] * state_in[k, 0:64, :].astype(F32)

    block = dp * 2 + sec
    attended[block] = mixed.astype(BF16).reshape(4, 16, HD)

    def send_attended(k, carry):
        rcopy(
            attended.at[block],
            attended.at[block],
            attended_sem.at[0],
            attended_sem.at[1],
            at_n((n + k) % 16),
        ).start()
        return carry

    lax.fori_loop(1, 16, send_attended, 0)
    am_advance(2)
    loads[2].wait()
    attended_all = rcopy(
        attended.at[fifteen], attended.at[fifteen], attended_sem.at[0], attended_sem.at[1], sibling
    )
    attended_all.wait_recv()
    partial = jnp.zeros((256, 512), F32)
    for h in range(4):
        partial = partial + jnp.dot(
            attended[:, h].reshape(256, HD),
            weight_v[h * HD : (h + 1) * HD, :],
            preferred_element_type=F32,
        )
    part_out[...] = partial.astype(BF16).reshape(16, 16, 512)

    def send_part(k, carry):
        dest = (mp + k) % 16
        rcopy(
            part_out.at[dest], part_in.at[mp], part_sem.at[0], part_sem.at[1], at_mp(dest)
        ).start()
        return carry

    lax.fori_loop(1, 16, send_part, 0)
    part_in[mp] = part_out[mp]
    am_advance(3)
    part_all = rcopy(
        part_out.at[fifteen], part_in.at[fifteen], part_sem.at[0], part_sem.at[1], sibling
    )
    part_all.wait_recv()
    hidden = resid[pl.ds(pl.multiple_of(mp * 16, 16), 16), :].astype(F32)
    projected = part_in[0].astype(F32)
    for k in range(1, 16):
        projected = projected + part_in[k].astype(F32)
    full[c, z, v, u] = (hidden + projected).astype(BF16)

    def send_one(k, carry):
        rcopy(
            full.at[c, z, v, u], full.at[c, z, v, u], one_sem.at[0], one_sem.at[1], at_z((z + k) % 8)
        ).start()
        return carry

    lax.fori_loop(1, 8, send_one, 0)
    am_advance(4)
    one_all = rcopy(
        full.at[c, pl.ds(0, 7), v, u],
        full.at[c, pl.ds(0, 7), v, u],
        one_sem.at[0],
        one_sem.at[1],
        sibling,
    )
    one_all.wait_recv()

    def send_two(k, carry):
        rcopy(
            full.at[c, :, v, u],
            full.at[c, :, v, u],
            two_sem.at[0],
            two_sem.at[1],
            at_uv((u + k) % 4, v),
        ).start()
        return carry

    lax.fori_loop(1, 4, send_two, 0)

    loads[3].wait()
    acc_a[...] = jnp.zeros_like(acc_a)
    acc_e[...] = jnp.zeros_like(acc_e)
    square_a[...] = jnp.zeros_like(square_a)
    square_e[...] = jnp.zeros_like(square_e)
    other = rcopy(amateur.at[c, 0], amateur.at[c, 0], am_rsend.at[0], am_rrecv.at[0], sibling)

    def am_block(k, carry):
        ref = amateur.at[1 - c, k]
        rcopy(ref, ref, am_rsend.at[k], am_rrecv.at[k], sibling).wait_recv()
        parts = []
        squares = square_a[...]
        for cc in range(2):
            wide = amateur[cc, k, 0:256, :].astype(F32)
            gain = amateur[cc, k, 256:272, :].astype(F32)[2:3]
            squares = squares + wide[:, 0:128] * wide[:, 0:128] + wide[:, 128:] * wide[:, 128:]
            parts.append((wide * gain).astype(BF16))
        square_a[...] = squares
        acc_a[...] += lax.dot_general(
            ha_v[:, pl.ds(pl.multiple_of(k * 512, 512), 512)],
            jnp.concatenate(parts, axis=1),
            NT,
            preferred_element_type=F32,
        )
        return carry

    lax.fori_loop(0, 8, am_block, 0)
    ones = jnp.ones((8, 128), F32)

    def inverse_norm(ref, width):
        sums = lax.dot_general(
            ones, ref[...], NT, preferred_element_type=F32, precision=lax.Precision.HIGHEST
        )
        return lax.rsqrt(sums[0:1] / width + EPSILON)

    logits_a = acc_a[...] * inverse_norm(square_a, 4096.0)
    acc_a[...] = logits_a
    top_a = jnp.max(logits_a, axis=0, keepdims=True)
    total_a = jnp.sum(jnp.exp(logits_a - top_a), axis=0, keepdims=True)

    two_all = rcopy(
        full.at[c, :, v, pl.ds(0, 3)],
        full.at[c, :, v, pl.ds(0, 3)],
        two_sem.at[0],
        two_sem.at[1],
        sibling,
    )
    two_all.wait_recv()
    above, below = (v + 1) % 4, (v + 3) % 4

    def three(which, zz, vv, target):
        ref = full.at[c, zz, vv]
        return rcopy(
            ref, ref, three_send.at[which, zz], three_recv.at[which, zz], at_uv(u, target)
        )

    def send_three(zz):
        three(0, zz, v, above).start()
        three(1, zz, v, below).start()

    def relay(zz, cc):
        ref = full.at[cc, zz]
        return rcopy(ref, ref, relay_send.at[zz], relay_recv.at[zz], sibling)

    send_three(0)
    send_three(1)
    loads[4].wait()

    def gather_block(zz, carry):
        @pl.when(zz < 6)
        def _():
            send_three(zz + 2)

        @pl.when(zz < 8)
        def _():
            three(0, zz, below, above).wait_recv()
            three(1, zz, above, below).wait_recv()

            @pl.when(zz % 2 == 0)
            def _():
                three(2, zz, below, above).start()

            @pl.when(zz % 2 == 1)
            def _():
                three(2, zz, above, below).start()

        @pl.when((zz >= 1) & (zz < 9))
        def _():
            three(2, zz - 1, (v + 2) % 4, above).wait_recv()
            relay(zz - 1, c).start()

        @pl.when(zz >= 2)
        def _():
            k = zz - 2
            relay(k, 1 - c).wait_recv()
            parts = []
            squares = square_e[...]
            for cc in range(2):
                wide = full[cc, k]
                if cc == 0:
                    wide = jnp.swapaxes(wide, 0, 1)
                wide = wide.reshape(256, 512).astype(F32)
                tile = amateur[cc, k, 256:272, :].astype(F32)
                for half in range(2):
                    piece = wide[:, half * 256 : half * 256 + 256]
                    squares = (
                        squares
                        + piece[:, 0:128] * piece[:, 0:128]
                        + piece[:, 128:] * piece[:, 128:]
                    )
                    parts.append((piece * tile[half : half + 1]).astype(BF16))
            square_e[...] = squares
            acc_e[...] += lax.dot_general(
                he_v[:, pl.ds(pl.multiple_of(k * 1024, 1024), 1024)],
                jnp.concatenate(parts, axis=1),
                NT,
                preferred_element_type=F32,
            )

        return carry

    lax.fori_loop(0, 10, gather_block, 0)

    logits_e = acc_e[...] * inverse_norm(square_e, 8192.0)
    top_e = jnp.max(logits_e, axis=0, keepdims=True)
    total_e = jnp.sum(jnp.exp(logits_e - top_e), axis=0, keepdims=True)
    difference = logits_e - CONTRAST * acc_a[...]
    pick_row = (iota((64, 256), 1) // 4 == iota((64, 256), 0)).astype(F32)
    step_row = iota((8, 256), 1) % 4 == iota((8, 256), 0)
    spread = jnp.dot(
        chosen[...].astype(F32),
        pick_row,
        preferred_element_type=F32,
        precision=lax.Precision.HIGHEST,
    )
    target = jnp.sum(jnp.where(step_row[0:4], spread, 0.0), axis=0, keepdims=True)
    target = target - ((n * 16 + mp) * 512).astype(F32)
    matched = iota((512, 256), 0).astype(F32) == target
    picked = jnp.sum(jnp.where(matched, difference, 0.0), axis=0, keepdims=True)

    row8 = iota((8, 256), 0)

    def pack(rows):
        tile = jnp.zeros((8, 256), F32)
        for k, row in enumerate(rows):
            tile = jnp.where(row8 == k, row, tile)
        return tile

    def join(ref):
        tiles = [ref[k] for k in range(16)]
        top = tiles[0]
        for k in range(1, 16):
            top = jnp.maximum(top, tiles[k])
        te, ta = top[0:1], top[2:3]
        se, sa, pick = jnp.zeros((1, 256), F32), jnp.zeros((1, 256), F32), jnp.zeros((1, 256), F32)
        for k in range(16):
            se = se + tiles[k][1:2] * jnp.exp(tiles[k][0:1] - te)
            sa = sa + tiles[k][3:4] * jnp.exp(tiles[k][2:3] - ta)
            pick = pick + tiles[k][4:5]
        return te, se, ta, sa, pick

    stats_p[mp] = pack((top_e, total_e, top_a, total_a, picked))

    def send_p(k, carry):
        rcopy(
            stats_p.at[mp], stats_p.at[mp], stats_sem.at[0], stats_sem.at[1], at_mp((mp + k) % 16)
        ).start()
        return carry

    lax.fori_loop(1, 16, send_p, 0)
    diff[...] = difference.T
    p_all = rcopy(
        stats_p.at[fifteen], stats_p.at[fifteen], stats_sem.at[0], stats_sem.at[1], sibling
    )
    p_all.wait_recv()
    stats_z[n] = pack(join(stats_p))

    def send_z(k, carry):
        rcopy(
            stats_z.at[n], stats_z.at[n], stats_sem.at[2], stats_sem.at[3], at_n((n + k) % 16)
        ).start()
        return carry

    lax.fori_loop(1, 16, send_z, 0)

    state_all.wait_send()
    attended_all.wait_send()
    part_all.wait_send()
    one_all.wait_send()
    two_all.wait_send()
    p_all.wait_send()
    for step in range(1, 5):
        am_copy(0, step).wait_send()
        if step < 4:
            am_copy(1, step).wait_send()

    def drain(k, carry):
        relay(k, c).wait_send()
        am_relay(k).wait_send()
        for which in range(3):
            three(which, k, v, above).wait_send()
        return carry

    lax.fori_loop(0, 8, drain, 0)
    z_all = rcopy(
        stats_z.at[fifteen], stats_z.at[fifteen], stats_sem.at[2], stats_sem.at[3], sibling
    )
    z_all.wait_recv()
    te, se, ta, sa, pick = join(stats_z)
    shift = te + jnp.log(se) - CONTRAST * (ta + jnp.log(sa))
    shift_t = jnp.where(iota((128, 256), 0) == 0, shift, 0.0).T
    out[...] = (diff[...] - shift_t[:, 0:1]).astype(BF16)
    masked = jnp.where(step_row, pick - shift, 0.0)
    out_chosen[...] = lax.dot_general(
        masked, pick_row, NT, preferred_element_type=F32, precision=lax.Precision.HIGHEST
    )[0:4]
    z_all.wait_send()


def local(
    queries,
    new_keys,
    new_values,
    cache_keys,
    cache_values,
    lengths,
    out_weight,
    resid_expert,
    gain_expert,
    hidden_amateur,
    gain_amateur,
    head_expert,
    head_amateur,
    chosen,
):
    vmem = pl.BlockSpec(memory_space=pltpu.VMEM)
    hbm = pl.BlockSpec(memory_space=pl.ANY)
    dma = pltpu.SemaphoreType.DMA
    scores, chosen_score = pl.pallas_call(
        kernel,
        out_shape=(
            jax.ShapeDtypeStruct((256, 512), BF16),
            jax.ShapeDtypeStruct((4, 64), F32),
        ),
        in_specs=[pl.BlockSpec(memory_space=pltpu.SMEM)] + [vmem] * 8 + [hbm] * 5,
        out_specs=(vmem, vmem),
        scratch_shapes=[
            pltpu.VMEM((4, 32, 1024), BF16),
            pltpu.VMEM((4, 32, 1024), BF16),
            pltpu.VMEM((512, 512), BF16),
            pltpu.VMEM((512, 8192), BF16),
            pltpu.VMEM((512, 4096), BF16),
            pltpu.VMEM((16, 80, 128), BF16),
            pltpu.VMEM((16, 80, 128), BF16),
            pltpu.VMEM((128, 128), F32),
            pltpu.VMEM((16, 4, 16, 128), BF16),
            pltpu.VMEM((16, 16, 512), BF16),
            pltpu.VMEM((16, 16, 512), BF16),
            pltpu.VMEM((2, 8, 4, 4, 16, 512), BF16),
            pltpu.VMEM((2, 8, 272, 256), BF16),
            pltpu.VMEM((512, 256), F32),
            pltpu.VMEM((512, 256), F32),
            pltpu.VMEM((256, 128), F32),
            pltpu.VMEM((256, 128), F32),
            pltpu.VMEM((256, 512), F32),
            pltpu.VMEM((16, 8, 256), F32),
            pltpu.VMEM((16, 8, 256), F32),
            dma((5,)),
            dma((2,)),
            dma((2,)),
            dma((2,)),
            dma((2,)),
            dma((2,)),
            dma((3, 8)),
            dma((3, 8)),
            dma((8,)),
            dma((8,)),
            dma((2, 5)),
            dma((2, 5)),
            dma((8,)),
            dma((8,)),
            dma((4,)),
        ],
        compiler_params=pltpu.CompilerParams(
            collective_id=0, has_side_effects=True, vmem_limit_bytes=56 * 1024 * 1024
        ),
        name="contrast",
    )(
        lengths,
        queries,
        new_keys,
        new_values,
        resid_expert,
        gain_expert.reshape(1, -1),
        gain_amateur.reshape(1, -1),
        hidden_amateur,
        chosen.T,
        cache_keys,
        cache_values,
        out_weight,
        head_expert,
        head_amateur,
    )
    return scores.reshape(64, 4, 512), chosen_score.T


def solution(mesh):
    return jax.shard_map(
        local,
        mesh=mesh,
        in_specs=(
            P("dp", None, None),
            P("dp", None, None),
            P("dp", None, None),
            P("dp", "mp", None),
            P("dp", "mp", None),
            P("dp"),
            P("mp", ("section", "dp")),
            P(None, ("section", "dp")),
            P(("section", "dp")),
            P(None, ("section", "dp")),
            P(("section", "dp")),
            P(("section", "dp", "mp"), None),
            P(("section", "dp", "mp"), None),
            P(),
        ),
        out_specs=(P(None, None, ("section", "dp", "mp")), P()),
        check_vma=False,
    )
```

```python
import jax
import jax.numpy as jnp
from jax import lax
from jax.experimental import pallas as pl
from jax.experimental.pallas import tpu as pltpu
from jax.sharding import PartitionSpec as P

MESH = pl.DeviceIdType.MESH
F32 = jnp.float32
BF16 = jnp.bfloat16
KVH = 8
HD = 128
CONTRAST = 0.5
NEGATIVE = -1e30
EPSILON = 1e-05
NT = (((1,), (1,)), ((), ()))
TN = (((0,), (0,)), ((), ()))


def rcopy(src, dst, send_sem, recv_sem, device):
    return pltpu.make_async_remote_copy(
        src_ref=src,
        dst_ref=dst,
        send_sem=send_sem,
        recv_sem=recv_sem,
        device_id=device,
        device_id_type=MESH,
    )


def iota(shape, dim):
    return lax.broadcasted_iota(jnp.int32, shape, dim)


def kernel(
    lengths,
    queries,
    new_keys,
    new_values,
    resid,
    gain_expert,
    gain_amateur,
    hidden_amateur,
    chosen,
    cache_keys,
    cache_values,
    out_weight,
    head_expert,
    head_amateur,
    out,
    out_chosen,
    keys_v,
    values_v,
    weight_v,
    he_v,
    ha_v,
    state_out,
    state_in,
    scale_t,
    attended,
    part_out,
    part_in,
    full,
    amateur,
    acc_e,
    acc_a,
    square_e,
    square_a,
    diff,
    stats_s,
    stats_h,
    stats_p,
    stats_z,
    stats_f,
    load_sem,
    state_sem,
    attended_sem,
    part_sem,
    one_send,
    one_recv,
    two_send,
    two_recv,
    three_send,
    three_recv,
    relay_send,
    relay_recv,
    am_send,
    am_recv,
    stats_send,
    stats_recv,
):
    sec = lax.axis_index("section")
    dp = lax.axis_index("dp")
    mp = lax.axis_index("mp")
    z = sec * 4 + dp // 2
    c = dp % 2
    n = sec * 8 + dp
    x, y = mp // 4, mp % 4
    u = x * (1 - c) + y * c
    v = y * (1 - c) + x * c

    def at_n(k):
        return (k // 8, k % 8, mp)

    def at_z(zz):
        return (zz // 4, (zz % 4) * 2 + c, mp)

    def at_mp(k):
        return (sec, dp, k)

    def at_uv(uu, vv):
        return (sec, dp, (uu * 4 + vv) * (1 - c) + (vv * 4 + uu) * c)

    sibling = (sec, dp + 1 - 2 * c, mp)

    loads = [
        pltpu.make_async_copy(cache_keys.at[pl.ds(sec * 4, 4)], keys_v, load_sem.at[0]),
        pltpu.make_async_copy(cache_values.at[pl.ds(sec * 4, 4)], values_v, load_sem.at[1]),
        pltpu.make_async_copy(out_weight, weight_v, load_sem.at[2]),
        pltpu.make_async_copy(head_amateur, ha_v, load_sem.at[3]),
        pltpu.make_async_copy(head_expert, he_v, load_sem.at[4]),
    ]

    barrier = pltpu.get_barrier_semaphore()

    def greet_mp(k, carry):
        pl.semaphore_signal(
            barrier, inc=1, device_id=at_mp((mp + k) % 16), device_id_type=MESH
        )
        return carry

    def greet_z(k, carry):
        pl.semaphore_signal(
            barrier, inc=1, device_id=at_z((z + k) % 8), device_id_type=MESH
        )
        return carry

    lax.fori_loop(1, 8, greet_z, 0)
    lax.fori_loop(1, 16, greet_mp, 0)
    pl.semaphore_signal(barrier, inc=1, device_id=sibling, device_id_type=MESH)
    for load in loads:
        load.start()

    amateur[c, z, u, 0:64, :] = hidden_amateur[pl.ds(pl.multiple_of(u * 64, 64), 64), :]
    row16 = iota((16, 256), 0)
    gains = jnp.where(
        row16 == 0,
        gain_expert[0:256].astype(F32).reshape(1, 256),
        jnp.where(
            row16 == 1,
            gain_expert[256:512].astype(F32).reshape(1, 256),
            jnp.where(row16 == 2, gain_amateur[...].astype(F32).reshape(1, 256), 0.0),
        ),
    )
    amateur[c, z, u, 64:80, :] = gains.astype(BF16)

    row_i, col_i = iota((128, 128), 0), iota((128, 128), 1)
    limit = jnp.zeros((128, 128), jnp.int32)
    for r in range(4):
        limit = jnp.where(row_i // 32 == r, lengths[sec * 4 + r], limit)
    live_old = (row_i // 32 == (col_i // 4) % 4) & (row_i % 32 + mp * 32 < limit)
    row_n, col_n = iota((16, 128), 0), iota((16, 128), 1)
    live_new = (row_n // 4 == (col_n // 4) % 4) & (row_n % 4 <= col_n % 4) & (mp == 0)
    loads[0].wait()
    loads[1].wait()

    def stacked(ref, start):
        part = ref[pl.ds(sec * 4, 4), :, pl.ds(start, HD)].astype(F32)
        return jnp.concatenate([part[r] for r in range(4)], axis=0)

    def attend(i, carry):
        g = i
        base = pl.multiple_of(g * HD, HD)
        keys_old = keys_v[:, :, pl.ds(base, HD)].reshape(128, HD)
        values_old = values_v[:, :, pl.ds(base, HD)].reshape(128, HD)
        keys_new = stacked(new_keys, base).astype(BF16)
        values_new = stacked(new_values, base).astype(BF16)
        query = jnp.concatenate(
            [stacked(queries, pl.multiple_of(g * 1024 + h * HD, HD)) for h in range(8)], axis=0
        ).astype(BF16)
        scaling = 1.0 / HD**0.5
        s_old = lax.dot_general(keys_old, query, NT, preferred_element_type=F32) * scaling
        s_new = lax.dot_general(keys_new, query, NT, preferred_element_type=F32) * scaling
        s_old = jnp.where(live_old, s_old, NEGATIVE)
        s_new = jnp.where(live_new, s_new, NEGATIVE)
        top = jnp.maximum(
            jnp.max(s_old, axis=0, keepdims=True), jnp.max(s_new, axis=0, keepdims=True)
        )
        top = top.astype(BF16).astype(F32)
        p_old = jnp.where(live_old, jnp.exp(s_old - top), 0.0)
        p_new = jnp.where(live_new, jnp.exp(s_new - top), 0.0)
        total = jnp.sum(p_old, axis=0, keepdims=True) + jnp.sum(p_new, axis=0, keepdims=True)
        mix = lax.dot_general(
            p_old.astype(BF16), values_old, TN, preferred_element_type=F32
        ) + lax.dot_general(p_new.astype(BF16), values_new, TN, preferred_element_type=F32)
        high = total.astype(BF16).astype(F32)
        tile = jnp.where(
            row_n == 0,
            top,
            jnp.where(row_n == 1, high, jnp.where(row_n == 2, total - high, 0.0)),
        ).astype(BF16)
        mix = mix.astype(BF16)
        for e in range(2):
            state_out[2 * g + e, 0:64, :] = mix[e * 64 : e * 64 + 64]
            state_out[2 * g + e, 64:80, :] = tile
        return carry

    lax.fori_loop(0, 8, attend, 0)
    pl.semaphore_wait(barrier, 23)

    def send_state(k, carry):
        dest = (mp + k) % 16
        rcopy(
            state_out.at[dest], state_in.at[mp], state_sem.at[0], state_sem.at[1], at_mp(dest)
        ).start()
        return carry

    lax.fori_loop(1, 16, send_state, 0)

    def send_am(k, carry):
        ref = amateur.at[c, z, u]
        rcopy(ref, ref, am_send.at[0], am_recv.at[0], at_z((z + k) % 8)).start()
        return carry

    lax.fori_loop(1, 8, send_am, 0)
    state_in[mp] = state_out[mp]
    fifteen = pl.ds(0, 15)
    state_all = rcopy(
        state_out.at[fifteen], state_in.at[fifteen], state_sem.at[0], state_sem.at[1], sibling
    )
    state_all.wait_recv()

    tiles = [state_in[k, 64:80, :].astype(F32) for k in range(16)]
    top = tiles[0][0:1]
    for k in range(1, 16):
        top = jnp.maximum(top, tiles[k][0:1])
    total = jnp.zeros((1, 128), F32)
    weights = jnp.zeros((128, 128), F32)
    for k in range(16):
        scale = jnp.exp(tiles[k][0:1] - top)
        total = total + scale * (tiles[k][1:2] + tiles[k][2:3])
        weights = jnp.where(row_i == k, scale, weights)
    scale_t[...] = (weights / total).T
    own = scale_t[pl.ds(pl.multiple_of((mp % 2) * 64, 64), 64), :]
    mixed = jnp.zeros((64, HD), F32)
    for k in range(16):
        mixed = mixed + own[:, k : k + 1] * state_in[k, 0:64, :].astype(F32)

    attended[c, z] = mixed.astype(BF16).reshape(4, 16, HD)

    def send_attended(k, carry):
        ref = attended.at[c, z]
        rcopy(ref, ref, attended_sem.at[0], attended_sem.at[1], at_z((z + k) % 8)).start()
        return carry

    lax.fori_loop(1, 8, send_attended, 0)

    am_one = amateur.at[c, pl.ds(0, 7), u]
    am_first = rcopy(am_one, am_one, am_send.at[0], am_recv.at[0], sibling)
    am_first.wait_recv()

    def send_quarter(k, carry):
        ref = amateur.at[c, :, u, pl.ds(0, 64)]
        rcopy(ref, ref, am_send.at[1], am_recv.at[1], at_uv((u + k) % 4, v)).start()
        return carry

    lax.fori_loop(1, 4, send_quarter, 0)
    loads[2].wait()
    seven = attended.at[c, pl.ds(0, 7)]
    attended_all = rcopy(seven, seven, attended_sem.at[0], attended_sem.at[1], sibling)
    attended_all.wait_recv()

    def pass_attended(cc):
        ref = attended.at[cc]
        return rcopy(ref, ref, attended_sem.at[2], attended_sem.at[3], sibling)

    pass_attended(c).start()

    def project(cc):
        partial = jnp.zeros((128, 512), F32)
        for h in range(4):
            partial = partial + jnp.dot(
                attended[cc, :, h].reshape(128, HD),
                weight_v[h * HD : (h + 1) * HD, :],
                preferred_element_type=F32,
            )
        part_out[cc] = partial.astype(BF16).reshape(8, 16, 512)

        def send_part(zz, carry):
            dest = (zz % 4) * 4 + cc * 2 + zz // 4

            @pl.when(dest != mp)
            def _():
                rcopy(
                    part_out.at[cc, zz], part_in.at[mp], part_sem.at[0], part_sem.at[1], at_mp(dest)
                ).start()

            return carry

        lax.fori_loop(0, 8, send_part, 0)

    project(c)
    pass_attended(1 - c).wait_recv()
    project(1 - c)
    part_in[mp] = part_out[(mp // 2) % 2, (mp % 2) * 4 + mp // 4]

    am_two = amateur.at[c, :, pl.ds(0, 3), pl.ds(0, 64)]
    am_second = rcopy(am_two, am_two, am_send.at[1], am_recv.at[1], sibling)
    am_second.wait_recv()

    def am_pass(cc):
        ref = amateur.at[cc]
        return rcopy(ref, ref, am_send.at[2], am_recv.at[2], sibling)

    am_pass(c).start()
    part_all = rcopy(
        part_in.at[fifteen], part_in.at[fifteen], part_sem.at[0], part_sem.at[1], sibling
    )
    part_all.wait_recv()
    hidden = resid[pl.ds(pl.multiple_of(mp * 16, 16), 16), :].astype(F32)
    projected = part_in[0].astype(F32)
    for k in range(1, 16):
        projected = projected + part_in[k].astype(F32)
    full[c, z, v, u] = (hidden + projected).astype(BF16)

    def one(block, target):
        ref = full.at[c, block, v, u]
        return rcopy(ref, ref, one_send, one_recv.at[block], at_z(target))

    def send_one(k, carry):
        one(z, (z + k) % 8).start()
        return carry

    lax.fori_loop(1, 8, send_one, 0)

    def two(half, k):
        ref = full.at[c, pl.ds(half * 4, 4), v, u]
        return rcopy(
            ref, ref, two_send.at[half], two_recv.at[half], at_uv((u + k) % 4, v)
        )

    def three(k, zz, vv):
        ref = full.at[c, zz, vv]
        return rcopy(
            ref, ref, three_send.at[zz], three_recv.at[k, zz], at_uv(u, (v + k) % 4)
        )

    def relay(zz, cc):
        ref = full.at[cc, zz]
        return rcopy(ref, ref, relay_send.at[zz], relay_recv.at[zz], sibling)

    for half in range(2):

        def wait_one(zz, carry):
            @pl.when(zz != z)
            def _():
                one(zz, z).wait_recv()

            return carry

        lax.fori_loop(half * 4, half * 4 + 4, wait_one, 0)
        for k in range(1, 4):
            two(half, k).start()

    def two_all(half):
        ref = full.at[c, pl.ds(half * 4, 4), v, pl.ds(0, 3)]
        return rcopy(ref, ref, two_send.at[half], two_recv.at[half], sibling)

    for half in range(2):
        two_all(half).wait_recv()

        def send_three(zz, carry):
            for k in (2, 1, 3):
                three(k, zz, v).start()
            return carry

        lax.fori_loop(half * 4, half * 4 + 4, send_three, 0)

    loads[3].wait()
    acc_a[...] = jnp.zeros_like(acc_a)
    acc_e[...] = jnp.zeros_like(acc_e)
    square_a[...] = jnp.zeros_like(square_a)
    square_e[...] = jnp.zeros_like(square_e)
    am_pass(1 - c).wait_recv()

    def am_block(k, carry):
        parts = []
        squares = square_a[...]
        for cc in range(2):
            wide = amateur[cc, k, :, 0:64, :].reshape(256, 256).astype(F32)
            gain = amateur[cc, k, x if cc == 0 else y, 64:80, :].astype(F32)[2:3]
            squares = squares + wide[:, 0:128] * wide[:, 0:128] + wide[:, 128:] * wide[:, 128:]
            parts.append((wide * gain).astype(BF16))
        square_a[...] = squares
        acc_a[...] += lax.dot_general(
            ha_v[:, pl.ds(pl.multiple_of(k * 512, 512), 512)],
            jnp.concatenate(parts, axis=1),
            NT,
            preferred_element_type=F32,
        )
        return carry

    lax.fori_loop(0, 8, am_block, 0)
    ones = jnp.ones((8, 128), F32)

    def inverse_norm(ref, width):
        sums = lax.dot_general(
            ones, ref[...], NT, preferred_element_type=F32, precision=lax.Precision.HIGHEST
        )
        return lax.rsqrt(sums[0:1] / width + EPSILON)

    logits_a = acc_a[...] * inverse_norm(square_a, 4096.0)
    acc_a[...] = logits_a
    top_a = jnp.max(logits_a, axis=0, keepdims=True)
    total_a = jnp.sum(jnp.exp(logits_a - top_a), axis=0, keepdims=True)

    loads[4].wait()

    def gather_block(zz, carry):
        @pl.when(zz < 8)
        def _():
            for k in (1, 3, 2):
                three(k, zz, (v - k + 4) % 4).wait_recv()
            relay(zz, c).start()

        @pl.when(zz >= 1)
        def _():
            k = zz - 1
            relay(k, 1 - c).wait_recv()
            parts = []
            squares = square_e[...]
            for cc in range(2):
                wide = full[cc, k]
                if cc == 0:
                    wide = jnp.swapaxes(wide, 0, 1)
                wide = wide.reshape(256, 512).astype(F32)
                tile = amateur[cc, k, x if cc == 0 else y, 64:80, :].astype(F32)
                for half in range(2):
                    piece = wide[:, half * 256 : half * 256 + 256]
                    squares = (
                        squares
                        + piece[:, 0:128] * piece[:, 0:128]
                        + piece[:, 128:] * piece[:, 128:]
                    )
                    parts.append((piece * tile[half : half + 1]).astype(BF16))
            square_e[...] = squares
            acc_e[...] += lax.dot_general(
                he_v[:, pl.ds(pl.multiple_of(k * 1024, 1024), 1024)],
                jnp.concatenate(parts, axis=1),
                NT,
                preferred_element_type=F32,
            )

        return carry

    lax.fori_loop(0, 9, gather_block, 0)

    logits_e = acc_e[...] * inverse_norm(square_e, 8192.0)
    top_e = jnp.max(logits_e, axis=0, keepdims=True)
    total_e = jnp.sum(jnp.exp(logits_e - top_e), axis=0, keepdims=True)
    difference = logits_e - CONTRAST * acc_a[...]
    pick_row = (iota((64, 256), 1) // 4 == iota((64, 256), 0)).astype(F32)
    step_row = iota((8, 256), 1) % 4 == iota((8, 256), 0)
    spread = jnp.dot(
        chosen[...].astype(F32),
        pick_row,
        preferred_element_type=F32,
        precision=lax.Precision.HIGHEST,
    )
    target = jnp.sum(jnp.where(step_row[0:4], spread, 0.0), axis=0, keepdims=True)
    target = target - ((n * 16 + mp) * 512).astype(F32)
    matched = iota((512, 256), 0).astype(F32) == target
    picked = jnp.sum(jnp.where(matched, difference, 0.0), axis=0, keepdims=True)

    row8 = iota((8, 128), 0)

    def pack(rows, half):
        tile = jnp.zeros((8, 128), F32)
        for k, row in enumerate(rows):
            tile = jnp.where(row8 == k, row[:, half * 128 : half * 128 + 128], tile)
        return tile

    def join(tiles):
        top = tiles[0]
        for tile in tiles[1:]:
            top = jnp.maximum(top, tile)
        te, ta = top[0:1], top[2:3]
        zero = jnp.zeros((1, 128), F32)
        se, sa, pick = zero, zero, zero
        for tile in tiles:
            se = se + tile[1:2] * jnp.exp(tile[0:1] - te)
            sa = sa + tile[3:4] * jnp.exp(tile[2:3] - ta)
            pick = pick + tile[4:5]
        return te, se, ta, sa, pick

    mine = (top_e, total_e, top_a, total_a, picked)
    stats_h[0] = pack(mine, 0)
    stats_h[1] = pack(mine, 1)
    pair = rcopy(stats_h.at[1 - c], stats_s, stats_send.at[0], stats_recv.at[0], sibling)
    pair.start()
    pair.wait_recv()
    stats_p[mp] = pack(join([stats_h[c], stats_s[...]]), 0)

    def send_p(k, carry):
        ref = stats_p.at[mp]
        rcopy(ref, ref, stats_send.at[1], stats_recv.at[1], at_mp((mp + k) % 16)).start()
        return carry

    lax.fori_loop(1, 16, send_p, 0)
    diff[...] = difference.T

    state_all.wait_send()
    attended_all.wait_send()
    pass_attended(c).wait_send()
    am_first.wait_send()
    am_second.wait_send()
    am_pass(c).wait_send()
    part_all.wait_send()
    ref = full.at[c, pl.ds(0, 7), v, u]
    rcopy(ref, ref, one_send, one_recv.at[0], sibling).wait_send()
    for half in range(2):
        two_all(half).wait_send()

    def drain(k, carry):
        relay(k, c).wait_send()
        ref = full.at[c, k, pl.ds(0, 3)]
        rcopy(ref, ref, three_send.at[k], three_recv.at[1, k], sibling).wait_send()
        return carry

    lax.fori_loop(0, 8, drain, 0)
    pair.wait_send()
    ref = stats_p.at[fifteen]
    p_all = rcopy(ref, ref, stats_send.at[1], stats_recv.at[1], sibling)
    p_all.wait_recv()
    stats_z[z] = pack(join([stats_p[k] for k in range(16)]), 0)

    def send_z(k, carry):
        ref = stats_z.at[z]
        rcopy(ref, ref, stats_send.at[2], stats_recv.at[2], at_z((z + k) % 8)).start()
        return carry

    lax.fori_loop(1, 8, send_z, 0)
    p_all.wait_send()
    ref = stats_z.at[pl.ds(0, 7)]
    z_all = rcopy(ref, ref, stats_send.at[2], stats_recv.at[2], sibling)
    z_all.wait_recv()
    te, se, ta, sa, pick = join([stats_z[k] for k in range(8)])
    shift = te + jnp.log(se) - CONTRAST * (ta + jnp.log(sa))
    stats_f[c] = pack((shift, pick - shift), 0)
    last = rcopy(stats_f.at[c], stats_f.at[c], stats_send.at[3], stats_recv.at[3], sibling)
    last.start()
    z_all.wait_send()
    last.wait_recv()
    both = jnp.concatenate([stats_f[0], stats_f[1]], axis=1)
    shift_t = jnp.concatenate([both] * 16, axis=0).T
    out[...] = (diff[...] - shift_t[:, 0:1]).reshape(64, 4, 512).astype(BF16)
    masked = jnp.where(step_row, both[1:2], 0.0)
    out_chosen[...] = lax.dot_general(
        masked, pick_row, NT, preferred_element_type=F32, precision=lax.Precision.HIGHEST
    )[0:4]
    last.wait_send()


def finish(scores, chosen_score, out, out_chosen):
    out[...] = scores[...]
    out_chosen[...] = chosen_score[...]


def local(
    queries,
    new_keys,
    new_values,
    cache_keys,
    cache_values,
    lengths,
    out_weight,
    resid_expert,
    gain_expert,
    hidden_amateur,
    gain_amateur,
    head_expert,
    head_amateur,
    chosen,
):
    vmem = pl.BlockSpec(memory_space=pltpu.VMEM)
    hbm = pl.BlockSpec(memory_space=pl.ANY)
    dma = pltpu.SemaphoreType.DMA
    scores, chosen_score = pl.pallas_call(
        kernel,
        out_shape=(
            jax.ShapeDtypeStruct((64, 4, 512), BF16),
            jax.ShapeDtypeStruct((4, 64), F32),
        ),
        in_specs=[pl.BlockSpec(memory_space=pltpu.SMEM)] + [vmem] * 8 + [hbm] * 5,
        out_specs=(vmem, vmem),
        scratch_shapes=[
            pltpu.VMEM((4, 32, 1024), BF16),
            pltpu.VMEM((4, 32, 1024), BF16),
            pltpu.VMEM((512, 512), BF16),
            pltpu.VMEM((512, 8192), BF16),
            pltpu.VMEM((512, 4096), BF16),
            pltpu.VMEM((16, 80, 128), BF16),
            pltpu.VMEM((16, 80, 128), BF16),
            pltpu.VMEM((128, 128), F32),
            pltpu.VMEM((2, 8, 4, 16, 128), BF16),
            pltpu.VMEM((2, 8, 16, 512), BF16),
            pltpu.VMEM((16, 16, 512), BF16),
            pltpu.VMEM((2, 8, 4, 4, 16, 512), BF16),
            pltpu.VMEM((2, 8, 4, 80, 256), BF16),
            pltpu.VMEM((512, 256), F32),
            pltpu.VMEM((512, 256), F32),
            pltpu.VMEM((256, 128), F32),
            pltpu.VMEM((256, 128), F32),
            pltpu.VMEM((256, 512), F32),
            pltpu.VMEM((8, 128), F32),
            pltpu.VMEM((2, 8, 128), F32),
            pltpu.VMEM((16, 8, 128), F32),
            pltpu.VMEM((8, 8, 128), F32),
            pltpu.VMEM((2, 8, 128), F32),
            dma((5,)),
            dma((2,)),
            dma((4,)),
            dma((2,)),
            dma,
            dma((8,)),
            dma((2,)),
            dma((2,)),
            dma((8,)),
            dma((4, 8)),
            dma((8,)),
            dma((8,)),
            dma((3,)),
            dma((3,)),
            dma((4,)),
            dma((4,)),
        ],
        compiler_params=pltpu.CompilerParams(
            collective_id=0, has_side_effects=True, vmem_limit_bytes=56 * 1024 * 1024
        ),
        name="contrast",
    )(
        lengths,
        queries,
        new_keys,
        new_values,
        resid_expert,
        gain_expert,
        gain_amateur,
        hidden_amateur,
        chosen.T,
        cache_keys,
        cache_values,
        out_weight,
        head_expert,
        head_amateur,
    )
    scores, chosen_score = pl.pallas_call(
        finish,
        out_shape=(
            jax.ShapeDtypeStruct((64, 4, 512), BF16),
            jax.ShapeDtypeStruct((4, 64), F32),
        ),
        in_specs=[vmem] * 2,
        out_specs=(vmem, vmem),
        name="finish",
    )(scores, chosen_score)
    return scores, chosen_score.T


def solution(mesh):
    return jax.shard_map(
        local,
        mesh=mesh,
        in_specs=(
            P("dp", None, None),
            P("dp", None, None),
            P("dp", None, None),
            P("dp", "mp", None),
            P("dp", "mp", None),
            P("dp"),
            P("mp", ("section", "dp")),
            P(None, ("section", "dp")),
            P(("section", "dp")),
            P(None, ("section", "dp")),
            P(("section", "dp")),
            P(("section", "dp", "mp"), None),
            P(("section", "dp", "mp"), None),
            P(),
        ),
        out_specs=(P(None, None, ("section", "dp", "mp")), P()),
        check_vma=False,
    )
```

```python
import jax
import jax.numpy as jnp
from jax import lax
from jax.experimental import pallas as pl
from jax.experimental.pallas import tpu as pltpu
from jax.sharding import PartitionSpec as P

MESH = pl.DeviceIdType.MESH
F32 = jnp.float32
BF16 = jnp.bfloat16
KVH = 8
HD = 128
CONTRAST = 0.5
NEGATIVE = -1e30
EPSILON = 1e-05
NT = (((1,), (1,)), ((), ()))
TN = (((0,), (0,)), ((), ()))


def rcopy(src, dst, send_sem, recv_sem, device):
    return pltpu.make_async_remote_copy(
        src_ref=src,
        dst_ref=dst,
        send_sem=send_sem,
        recv_sem=recv_sem,
        device_id=device,
        device_id_type=MESH,
    )


def iota(shape, dim):
    return lax.broadcasted_iota(jnp.int32, shape, dim)


def kernel(
    lengths,
    queries,
    new_keys,
    new_values,
    resid,
    gain_expert,
    gain_amateur,
    hidden_amateur,
    chosen,
    cache_keys,
    cache_values,
    out_weight,
    head_expert,
    head_amateur,
    out,
    out_chosen,
    keys_v,
    values_v,
    weight_v,
    he_v,
    ha_v,
    state_out,
    state_in,
    scale_t,
    attended,
    part_out,
    part_in,
    full,
    amateur,
    acc_e,
    acc_a,
    square_e,
    square_a,
    diff,
    stats_s,
    stats_p,
    stats_z,
    load_sem,
    state_sem,
    attended_sem,
    part_sem,
    one_send,
    one_recv,
    two_send,
    two_recv,
    three_send,
    three_recv,
    relay_send,
    relay_recv,
    am_send,
    am_recv,
    am_rsend,
    am_rrecv,
    stats_send,
    stats_recv,
):
    sec = lax.axis_index("section")
    dp = lax.axis_index("dp")
    mp = lax.axis_index("mp")
    z = sec * 4 + dp // 2
    c = dp % 2
    n = sec * 8 + dp
    x, y = mp // 4, mp % 4
    u = x * (1 - c) + y * c
    v = y * (1 - c) + x * c

    def at_n(k):
        return (k // 8, k % 8, mp)

    def at_z(zz):
        return (zz // 4, (zz % 4) * 2 + c, mp)

    def at_mp(k):
        return (sec, dp, k)

    def at_uv(uu, vv):
        return (sec, dp, (uu * 4 + vv) * (1 - c) + (vv * 4 + uu) * c)

    sibling = (sec, dp + 1 - 2 * c, mp)

    loads = [
        pltpu.make_async_copy(cache_keys.at[pl.ds(sec * 4, 4)], keys_v, load_sem.at[0]),
        pltpu.make_async_copy(cache_values.at[pl.ds(sec * 4, 4)], values_v, load_sem.at[1]),
        pltpu.make_async_copy(out_weight, weight_v, load_sem.at[2]),
        pltpu.make_async_copy(head_amateur, ha_v, load_sem.at[3]),
        pltpu.make_async_copy(head_expert, he_v, load_sem.at[4]),
    ]

    barrier = pltpu.get_barrier_semaphore()

    def greet_mp(k, carry):
        pl.semaphore_signal(
            barrier, inc=1, device_id=at_mp((mp + k) % 16), device_id_type=MESH
        )
        return carry

    def greet_n(k, carry):
        pl.semaphore_signal(
            barrier, inc=1, device_id=at_n((n + k) % 16), device_id_type=MESH
        )
        return carry

    lax.fori_loop(1, 16, greet_n, 0)
    lax.fori_loop(1, 16, greet_mp, 0)
    for load in loads:
        load.start()

    amateur[c, z, 0:256, :] = hidden_amateur[...]
    row16 = iota((16, 256), 0)
    gains = jnp.where(
        row16 == 0,
        gain_expert[0:256].astype(F32).reshape(1, 256),
        jnp.where(
            row16 == 1,
            gain_expert[256:512].astype(F32).reshape(1, 256),
            jnp.where(row16 == 2, gain_amateur[...].astype(F32).reshape(1, 256), 0.0),
        ),
    )
    amateur[c, z, 256:272, :] = gains.astype(BF16)

    row_i, col_i = iota((128, 128), 0), iota((128, 128), 1)
    limit = jnp.zeros((128, 128), jnp.int32)
    for r in range(4):
        limit = jnp.where(row_i // 32 == r, lengths[sec * 4 + r], limit)
    live_old = (row_i // 32 == (col_i // 4) % 4) & (row_i % 32 + mp * 32 < limit)
    row_n, col_n = iota((16, 128), 0), iota((16, 128), 1)
    live_new = (row_n // 4 == (col_n // 4) % 4) & (row_n % 4 <= col_n % 4) & (mp == 0)
    loads[0].wait()
    loads[1].wait()

    def stacked(ref, start):
        part = ref[pl.ds(sec * 4, 4), :, pl.ds(start, HD)].astype(F32)
        return jnp.concatenate([part[r] for r in range(4)], axis=0)

    def attend(i, carry):
        g = i
        base = pl.multiple_of(g * HD, HD)
        keys_old = keys_v[:, :, pl.ds(base, HD)].reshape(128, HD)
        values_old = values_v[:, :, pl.ds(base, HD)].reshape(128, HD)
        keys_new = stacked(new_keys, base).astype(BF16)
        values_new = stacked(new_values, base).astype(BF16)
        query = jnp.concatenate(
            [stacked(queries, pl.multiple_of(g * 1024 + h * HD, HD)) for h in range(8)], axis=0
        ).astype(BF16)
        scaling = 1.0 / HD**0.5
        s_old = lax.dot_general(keys_old, query, NT, preferred_element_type=F32) * scaling
        s_new = lax.dot_general(keys_new, query, NT, preferred_element_type=F32) * scaling
        s_old = jnp.where(live_old, s_old, NEGATIVE)
        s_new = jnp.where(live_new, s_new, NEGATIVE)
        top = jnp.maximum(
            jnp.max(s_old, axis=0, keepdims=True), jnp.max(s_new, axis=0, keepdims=True)
        )
        top = top.astype(BF16).astype(F32)
        p_old = jnp.where(live_old, jnp.exp(s_old - top), 0.0)
        p_new = jnp.where(live_new, jnp.exp(s_new - top), 0.0)
        total = jnp.sum(p_old, axis=0, keepdims=True) + jnp.sum(p_new, axis=0, keepdims=True)
        mix = lax.dot_general(
            p_old.astype(BF16), values_old, TN, preferred_element_type=F32
        ) + lax.dot_general(p_new.astype(BF16), values_new, TN, preferred_element_type=F32)
        high = total.astype(BF16).astype(F32)
        tile = jnp.where(
            row_n == 0,
            top,
            jnp.where(row_n == 1, high, jnp.where(row_n == 2, total - high, 0.0)),
        ).astype(BF16)
        mix = mix.astype(BF16)
        for e in range(2):
            state_out[2 * g + e, 0:64, :] = mix[e * 64 : e * 64 + 64]
            state_out[2 * g + e, 64:80, :] = tile
        return carry

    lax.fori_loop(0, 8, attend, 0)
    pl.semaphore_wait(barrier, 30)

    def send_state(k, carry):
        dest = (mp + k) % 16
        rcopy(
            state_out.at[dest], state_in.at[mp], state_sem.at[0], state_sem.at[1], at_mp(dest)
        ).start()
        return carry

    lax.fori_loop(1, 16, send_state, 0)

    def am_copy(way, step):
        if way == 0:
            shard, target = (z - step + 9) % 8, (z + 1) % 8
        else:
            shard, target = (z + step - 1) % 8, (z + 7) % 8
        ref = amateur.at[c, shard]
        return rcopy(ref, ref, am_send.at[way, step], am_recv.at[way, step], at_z(target))

    def am_relay(shard, cc):
        ref = amateur.at[cc, shard]
        return rcopy(ref, ref, am_rsend.at[shard], am_rrecv.at[shard], sibling)

    def am_advance(step):
        am_copy(0, step).wait_recv()
        if step < 4:
            am_copy(1, step).wait_recv()
            am_copy(0, step + 1).start()
            if step < 3:
                am_copy(1, step + 1).start()
            am_relay((z + step) % 8, c).start()
        am_relay((z - step + 8) % 8, c).start()

    am_copy(0, 1).start()
    am_copy(1, 1).start()
    am_relay(z, c).start()
    state_in[mp] = state_out[mp]
    fifteen = pl.ds(0, 15)
    state_all = rcopy(
        state_out.at[fifteen], state_in.at[fifteen], state_sem.at[0], state_sem.at[1], sibling
    )
    state_all.wait_recv()

    tiles = [state_in[k, 64:80, :].astype(F32) for k in range(16)]
    top = tiles[0][0:1]
    for k in range(1, 16):
        top = jnp.maximum(top, tiles[k][0:1])
    total = jnp.zeros((1, 128), F32)
    weights = jnp.zeros((128, 128), F32)
    for k in range(16):
        scale = jnp.exp(tiles[k][0:1] - top)
        total = total + scale * (tiles[k][1:2] + tiles[k][2:3])
        weights = jnp.where(row_i == k, scale, weights)
    scale_t[...] = (weights / total).T
    own = scale_t[pl.ds(pl.multiple_of((mp % 2) * 64, 64), 64), :]
    mixed = jnp.zeros((64, HD), F32)
    for k in range(16):
        mixed = mixed + own[:, k : k + 1] * state_in[k, 0:64, :].astype(F32)

    block = dp * 2 + sec
    attended[block] = mixed.astype(BF16).reshape(4, 16, HD)

    def send_attended(k, carry):
        ref = attended.at[block]
        rcopy(ref, ref, attended_sem.at[0], attended_sem.at[1], at_n((n + k) % 16)).start()
        return carry

    lax.fori_loop(1, 16, send_attended, 0)
    loads[2].wait()
    fifteen_a = attended.at[fifteen]
    attended_all = rcopy(fifteen_a, fifteen_a, attended_sem.at[0], attended_sem.at[1], sibling)
    attended_all.wait_recv()
    partial = jnp.zeros((256, 512), F32)
    for h in range(4):
        partial = partial + jnp.dot(
            attended[:, h].reshape(256, HD),
            weight_v[h * HD : (h + 1) * HD, :],
            preferred_element_type=F32,
        )
    part_out[...] = partial.astype(BF16).reshape(16, 16, 512)

    def send_part(k, carry):
        dest = (mp + k) % 16
        rcopy(
            part_out.at[dest], part_in.at[mp], part_sem.at[0], part_sem.at[1], at_mp(dest)
        ).start()
        return carry

    lax.fori_loop(1, 16, send_part, 0)
    part_in[mp] = part_out[mp]
    am_advance(1)
    part_all = rcopy(
        part_in.at[fifteen], part_in.at[fifteen], part_sem.at[0], part_sem.at[1], sibling
    )
    part_all.wait_recv()
    hidden = resid[pl.ds(pl.multiple_of(mp * 16, 16), 16), :].astype(F32)
    projected = part_in[0].astype(F32)
    for k in range(1, 16):
        projected = projected + part_in[k].astype(F32)
    full[c, 3, v, u] = (hidden + projected).astype(BF16)

    def one(slot, target):
        return rcopy(
            full.at[c, 3, v, u], full.at[c, slot, v, u], one_send, one_recv.at[slot], at_z(target)
        )

    def send_one(k, carry):
        one((11 - k) % 8, (z + k) % 8).start()
        return carry

    lax.fori_loop(1, 8, send_one, 0)

    def two(half, k):
        ref = full.at[c, pl.ds(half * 4, 4), v, u]
        return rcopy(
            ref, ref, two_send.at[half], two_recv.at[half], at_uv((u + k) % 4, v)
        )

    def three(k, zz, vv):
        ref = full.at[c, zz, vv]
        return rcopy(
            ref, ref, three_send.at[zz], three_recv.at[k, zz], at_uv(u, (v + k) % 4)
        )

    def relay(zz, cc):
        ref = full.at[cc, zz]
        return rcopy(ref, ref, relay_send.at[zz], relay_recv.at[zz], sibling)

    for half in range(2):

        def wait_one(zz, carry):
            @pl.when(zz != 3)
            def _():
                one(zz, z).wait_recv()

            return carry

        lax.fori_loop(half * 4, half * 4 + 4, wait_one, 0)
        for k in range(1, 4):
            two(half, k).start()

    am_advance(2)

    def two_all(half):
        ref = full.at[c, pl.ds(half * 4, 4), v, pl.ds(0, 3)]
        return rcopy(ref, ref, two_send.at[half], two_recv.at[half], sibling)

    def send_three(zz, carry):
        for k in (2, 1, 3):
            three(k, zz, v).start()
        return carry

    two_all(0).wait_recv()
    lax.fori_loop(0, 4, send_three, 0)
    am_advance(3)

    loads[3].wait()
    acc_a[...] = jnp.zeros_like(acc_a)
    acc_e[...] = jnp.zeros_like(acc_e)
    square_a[...] = jnp.zeros_like(square_a)
    square_e[...] = jnp.zeros_like(square_e)

    def am_block(j, carry):
        k = (z + 5 + j) % 8
        am_relay(k, 1 - c).wait_recv()
        parts = []
        squares = square_a[...]
        for cc in range(2):
            wide = amateur[cc, k, 0:256, :].astype(F32)
            gain = amateur[cc, k, 256:272, :].astype(F32)[2:3]
            squares = squares + wide[:, 0:128] * wide[:, 0:128] + wide[:, 128:] * wide[:, 128:]
            parts.append((wide * gain).astype(BF16))
        square_a[...] = squares
        acc_a[...] += lax.dot_general(
            ha_v[:, pl.ds(pl.multiple_of(k * 512, 512), 512)],
            jnp.concatenate(parts, axis=1),
            NT,
            preferred_element_type=F32,
        )
        return carry

    lax.fori_loop(0, 7, am_block, 0)
    ones = jnp.ones((8, 128), F32)

    def inverse_norm(ref, width):
        sums = lax.dot_general(
            ones, ref[...], NT, preferred_element_type=F32, precision=lax.Precision.HIGHEST
        )
        return lax.rsqrt(sums[0:1] / width + EPSILON)

    row8 = iota((8, 128), 0)

    def pack(rows):
        tile = jnp.zeros((8, 128), F32)
        for k, row in enumerate(rows):
            tile = jnp.where(row8 == k, row, tile)
        return tile

    def halves(rows):
        return pack([row[:, h * 128 : h * 128 + 128] for row in rows for h in range(2)])

    def join(tiles):
        top = tiles[0]
        for tile in tiles[1:]:
            top = jnp.maximum(top, tile)
        top = top[0:2]
        total, pick = jnp.zeros((2, 128), F32), jnp.zeros((2, 128), F32)
        for tile in tiles:
            total = total + tile[2:4] * jnp.exp(tile[0:2] - top)
            pick = pick + tile[4:6]
        return top, total, pick

    def joined(tiles):
        return pack([part[h : h + 1] for part in join(tiles) for h in range(2)])

    fifteen_p = stats_p.at[0, fifteen]
    seven_z = stats_z.at[0, pl.ds(0, 7)]

    def pair(which):
        return rcopy(
            stats_s.at[which, 0],
            stats_s.at[which, 1],
            stats_send.at[which, 0],
            stats_recv.at[which, 0],
            sibling,
        )

    def start_pair(which, rows):
        stats_s[which, 0] = halves(rows)
        pair(which).start()

    def start_p(which):
        pair(which).wait_recv()
        stats_p[which, mp] = joined([stats_s[which, 0], stats_s[which, 1]])

        def send_p(k, carry):
            ref = stats_p.at[which, mp]
            rcopy(
                ref, ref, stats_send.at[which, 1], stats_recv.at[which, 1], at_mp((mp + k) % 16)
            ).start()
            return carry

        lax.fori_loop(1, 16, send_p, 0)

    def p_all(which):
        return rcopy(
            fifteen_p, fifteen_p, stats_send.at[which, 1], stats_recv.at[which, 1], sibling
        )

    def start_z(which):
        p_all(which).wait_recv()
        stats_z[which, z] = joined([stats_p[which, k] for k in range(16)])

        def send_z(k, carry):
            ref = stats_z.at[which, z]
            rcopy(
                ref, ref, stats_send.at[which, 2], stats_recv.at[which, 2], at_z((z + k) % 8)
            ).start()
            return carry

        lax.fori_loop(1, 8, send_z, 0)

    def z_all(which):
        return rcopy(seven_z, seven_z, stats_send.at[which, 2], stats_recv.at[which, 2], sibling)

    def settle(which):
        pair(which).wait_send()
        p_all(which).wait_send()
        z_all(which).wait_send()

    two_all(1).wait_recv()
    loads[4].wait()

    def gather_block(zz, carry):
        @pl.when(zz < 8)
        def _():
            for k in (1, 3, 2):
                three(k, zz, (v - k + 4) % 4).wait_recv()
            relay(zz, c).start()

            @pl.when(zz < 4)
            def _():
                send_three(zz + 4, 0)


        @pl.when(zz >= 1)
        def _():
            k = zz - 1
            relay(k, 1 - c).wait_recv()
            parts = []
            squares = square_e[...]
            for cc in range(2):
                wide = full[cc, k]
                if cc == 0:
                    wide = jnp.swapaxes(wide, 0, 1)
                wide = wide.reshape(256, 512).astype(F32)
                tile = amateur[cc, (z + 5 + k) % 8, 256:272, :].astype(F32)
                for half in range(2):
                    piece = wide[:, half * 256 : half * 256 + 256]
                    squares = (
                        squares
                        + piece[:, 0:128] * piece[:, 0:128]
                        + piece[:, 128:] * piece[:, 128:]
                    )
                    parts.append((piece * tile[half : half + 1]).astype(BF16))
            square_e[...] = squares
            acc_e[...] += lax.dot_general(
                he_v[:, pl.ds(pl.multiple_of((z + 5 + k) % 8 * 1024, 1024), 1024)],
                jnp.concatenate(parts, axis=1),
                NT,
                preferred_element_type=F32,
            )

        return carry

    lax.fori_loop(0, 3, gather_block, 0)
    am_advance(4)
    lax.fori_loop(3, 4, gather_block, 0)
    lax.fori_loop(7, 8, am_block, 0)
    logits_a = acc_a[...] * inverse_norm(square_a, 4096.0)
    acc_a[...] = logits_a
    top_a = jnp.max(logits_a, axis=0, keepdims=True)
    total_a = jnp.sum(jnp.exp(logits_a - top_a), axis=0, keepdims=True)
    start_pair(1, (top_a, total_a))
    lax.fori_loop(4, 6, gather_block, 0)
    start_p(1)
    lax.fori_loop(6, 9, gather_block, 0)

    logits_e = acc_e[...] * inverse_norm(square_e, 8192.0)
    top_e = jnp.max(logits_e, axis=0, keepdims=True)
    total_e = jnp.sum(jnp.exp(logits_e - top_e), axis=0, keepdims=True)
    difference = logits_e - CONTRAST * acc_a[...]
    pick_row = (iota((64, 256), 1) // 4 == iota((64, 256), 0)).astype(F32)
    step_row = iota((8, 256), 1) % 4 == iota((8, 256), 0)
    spread = jnp.dot(
        chosen[...].astype(F32),
        pick_row,
        preferred_element_type=F32,
        precision=lax.Precision.HIGHEST,
    )
    target = jnp.sum(jnp.where(step_row[0:4], spread, 0.0), axis=0, keepdims=True)
    target = target - ((n * 16 + mp) * 512).astype(F32)
    matched = iota((512, 256), 0).astype(F32) == target
    picked = jnp.sum(jnp.where(matched, difference, 0.0), axis=0, keepdims=True)

    start_pair(0, (top_e, total_e, picked))
    start_p(0)
    start_z(1)
    diff[...] = difference.T

    state_all.wait_send()
    attended_all.wait_send()
    for step in range(1, 5):
        am_copy(0, step).wait_send()
        if step < 4:
            am_copy(1, step).wait_send()
    part_all.wait_send()
    ref = full.at[c, pl.ds(0, 7), v, u]
    rcopy(ref, ref, one_send, one_recv.at[0], sibling).wait_send()
    for half in range(2):
        two_all(half).wait_send()

    def drain(k, carry):
        relay(k, c).wait_send()
        am_relay(k, c).wait_send()
        ref = full.at[c, k, pl.ds(0, 3)]
        rcopy(ref, ref, three_send.at[k], three_recv.at[1, k], sibling).wait_send()
        return carry

    lax.fori_loop(0, 8, drain, 0)
    start_z(0)
    settle(1)
    z_all(1).wait_recv()
    top, total, _ = join([stats_z[1, k] for k in range(8)])
    lse_a = top + jnp.log(total)
    z_all(0).wait_recv()
    top, total, pick = join([stats_z[0, k] for k in range(8)])
    shift = top + jnp.log(total) - CONTRAST * lse_a
    chosen_row = pick - shift
    shift = jnp.concatenate([shift[0:1], shift[1:2]], axis=1)
    chosen_row = jnp.concatenate([chosen_row[0:1], chosen_row[1:2]], axis=1)
    shift_t = jnp.broadcast_to(shift, (128, 256)).T
    out[...] = (diff[...] - shift_t[:, 0:1]).reshape(64, 4, 512).astype(BF16)
    masked = jnp.where(step_row, chosen_row, 0.0)
    out_chosen[...] = lax.dot_general(
        masked, pick_row, NT, preferred_element_type=F32, precision=lax.Precision.HIGHEST
    )[0:4]
    settle(0)


def finish(scores, chosen_score, out, out_chosen):
    out[...] = scores[...]
    out_chosen[...] = chosen_score[...]


def local(
    queries,
    new_keys,
    new_values,
    cache_keys,
    cache_values,
    lengths,
    out_weight,
    resid_expert,
    gain_expert,
    hidden_amateur,
    gain_amateur,
    head_expert,
    head_amateur,
    chosen,
):
    vmem = pl.BlockSpec(memory_space=pltpu.VMEM)
    hbm = pl.BlockSpec(memory_space=pl.ANY)
    dma = pltpu.SemaphoreType.DMA
    scores, chosen_score = pl.pallas_call(
        kernel,
        out_shape=(
            jax.ShapeDtypeStruct((64, 4, 512), BF16),
            jax.ShapeDtypeStruct((4, 64), F32),
        ),
        in_specs=[pl.BlockSpec(memory_space=pltpu.SMEM)] + [vmem] * 8 + [hbm] * 5,
        out_specs=(vmem, vmem),
        scratch_shapes=[
            pltpu.VMEM((4, 32, 1024), BF16),
            pltpu.VMEM((4, 32, 1024), BF16),
            pltpu.VMEM((512, 512), BF16),
            pltpu.VMEM((512, 8192), BF16),
            pltpu.VMEM((512, 4096), BF16),
            pltpu.VMEM((16, 80, 128), BF16),
            pltpu.VMEM((16, 80, 128), BF16),
            pltpu.VMEM((128, 128), F32),
            pltpu.VMEM((16, 4, 16, 128), BF16),
            pltpu.VMEM((16, 16, 512), BF16),
            pltpu.VMEM((16, 16, 512), BF16),
            pltpu.VMEM((2, 8, 4, 4, 16, 512), BF16),
            pltpu.VMEM((2, 8, 272, 256), BF16),
            pltpu.VMEM((512, 256), F32),
            pltpu.VMEM((512, 256), F32),
            pltpu.VMEM((256, 128), F32),
            pltpu.VMEM((256, 128), F32),
            pltpu.VMEM((256, 512), F32),
            pltpu.VMEM((2, 2, 8, 128), F32),
            pltpu.VMEM((2, 16, 8, 128), F32),
            pltpu.VMEM((2, 8, 8, 128), F32),
            dma((5,)),
            dma((2,)),
            dma((2,)),
            dma((2,)),
            dma,
            dma((8,)),
            dma((2,)),
            dma((2,)),
            dma((8,)),
            dma((4, 8)),
            dma((8,)),
            dma((8,)),
            dma((2, 5)),
            dma((2, 5)),
            dma((8,)),
            dma((8,)),
            dma((2, 3)),
            dma((2, 3)),
        ],
        compiler_params=pltpu.CompilerParams(
            collective_id=0, has_side_effects=True, vmem_limit_bytes=56 * 1024 * 1024
        ),
        name="contrast",
    )(
        lengths,
        queries,
        new_keys,
        new_values,
        resid_expert,
        gain_expert,
        gain_amateur,
        hidden_amateur,
        chosen.T,
        cache_keys,
        cache_values,
        out_weight,
        head_expert,
        head_amateur,
    )
    scores, chosen_score = pl.pallas_call(
        finish,
        out_shape=(
            jax.ShapeDtypeStruct((64, 4, 512), BF16),
            jax.ShapeDtypeStruct((4, 64), F32),
        ),
        in_specs=[vmem] * 2,
        out_specs=(vmem, vmem),
        name="finish",
    )(scores, chosen_score)
    return scores, chosen_score.T


def solution(mesh):
    return jax.shard_map(
        local,
        mesh=mesh,
        in_specs=(
            P("dp", None, None),
            P("dp", None, None),
            P("dp", None, None),
            P("dp", "mp", None),
            P("dp", "mp", None),
            P("dp"),
            P("mp", ("section", "dp")),
            P(None, ("section", "dp")),
            P(("section", "dp")),
            P(None, ("section", "dp")),
            P(("section", "dp")),
            P(("section", "dp", "mp"), None),
            P(("section", "dp", "mp"), None),
            P(),
        ),
        out_specs=(P(None, None, ("section", "dp", "mp")), P()),
        check_vma=False,
    )
```

```python
import jax
import jax.numpy as jnp
from jax import lax
from jax.experimental import pallas as pl
from jax.experimental.pallas import tpu as pltpu
from jax.sharding import PartitionSpec as P

MESH = pl.DeviceIdType.MESH
F32 = jnp.float32
BF16 = jnp.bfloat16
KVH = 8
HD = 128
CONTRAST = 0.5
NEGATIVE = -1e30
EPSILON = 1e-05
NT = (((1,), (1,)), ((), ()))
TN = (((0,), (0,)), ((), ()))


def rcopy(src, dst, send_sem, recv_sem, device):
    return pltpu.make_async_remote_copy(
        src_ref=src,
        dst_ref=dst,
        send_sem=send_sem,
        recv_sem=recv_sem,
        device_id=device,
        device_id_type=MESH,
    )


def iota(shape, dim):
    return lax.broadcasted_iota(jnp.int32, shape, dim)


def place(i):
    return (2 - i + 3 * (i // 2) + 2 * (i // 3)) % 4


def hop(k):
    return (4 + (k + 1) // 2 * (1 - 2 * (k % 2))) % 8


def kernel(
    lengths,
    queries,
    new_keys,
    new_values,
    resid,
    gain_expert,
    gain_amateur,
    hidden_amateur,
    chosen,
    cache_keys,
    cache_values,
    out_weight,
    head_expert,
    head_amateur,
    out,
    out_chosen,
    queries_v,
    new_keys_v,
    new_values_v,
    resid_v,
    keys_v,
    values_v,
    weight_v,
    he_v,
    ha_v,
    state_out,
    state_in,
    scale_t,
    attended,
    part_out,
    part_in,
    full,
    amateur,
    acc_e,
    acc_a,
    square_e,
    square_a,
    diff,
    stats_s,
    stats_p,
    stats_z,
    load_sem,
    state_sem,
    attended_sem,
    part_sem,
    one_send,
    one_recv,
    two_send,
    two_recv,
    three_send,
    three_recv,
    relay_send,
    relay_recv,
    am_send,
    am_recv,
    am_rsend,
    am_rrecv,
    stats_send,
    stats_recv,
):
    sec = lax.axis_index("section")
    dp = lax.axis_index("dp")
    mp = lax.axis_index("mp")
    z = sec * 4 + dp // 2
    c = dp % 2
    n = sec * 8 + dp
    x, y = mp // 4, mp % 4
    u = x * (1 - c) + y * c
    v = y * (1 - c) + x * c

    def at_n(k):
        return (k // 8, k % 8, mp)

    def at_z(zz):
        return (zz // 4, (zz % 4) * 2 + c, mp)

    def at_mp(k):
        return (sec, dp, k)

    def at_uv(uu, vv):
        return (sec, dp, (uu * 4 + vv) * (1 - c) + (vv * 4 + uu) * c)

    def far_mp(k):
        return (x + place(k % 4)) % 4 * 4 + (y + place(k // 4)) % 4

    def far_n(k):
        return (z + hop(k // 2)) % 8 * 2 + (c + 1 + k) % 2

    sibling = (sec, dp + 1 - 2 * c, mp)

    mine = pl.ds(sec * 4, 4)
    loads = [
        pltpu.make_async_copy(cache_keys.at[pl.ds(sec * 4, 4)], keys_v, load_sem.at[0]),
        pltpu.make_async_copy(cache_values.at[pl.ds(sec * 4, 4)], values_v, load_sem.at[1]),
        pltpu.make_async_copy(out_weight, weight_v, load_sem.at[2]),
        pltpu.make_async_copy(head_amateur, ha_v, load_sem.at[3]),
        pltpu.make_async_copy(head_expert, he_v, load_sem.at[4]),
        pltpu.make_async_copy(
            resid.at[pl.ds(pl.multiple_of(mp * 16, 16), 16)], resid_v, load_sem.at[5]
        ),
    ]
    first_loads = [
        pltpu.make_async_copy(queries.at[mine], queries_v, load_sem.at[6]),
        pltpu.make_async_copy(new_keys.at[mine], new_keys_v, load_sem.at[7]),
        pltpu.make_async_copy(new_values.at[mine], new_values_v, load_sem.at[8]),
        pltpu.make_async_copy(hidden_amateur, amateur.at[c, z, pl.ds(0, 256)], load_sem.at[9]),
    ]

    barrier = pltpu.get_barrier_semaphore()

    def greet_mp(k, carry):
        pl.semaphore_signal(
            barrier, inc=1, device_id=at_mp(far_mp(k)), device_id_type=MESH
        )
        return carry

    def greet_n(k, carry):
        pl.semaphore_signal(
            barrier, inc=1, device_id=at_n(far_n(k)), device_id_type=MESH
        )
        return carry

    lax.fori_loop(0, 15, greet_n, 0)
    lax.fori_loop(0, 15, greet_mp, 0)
    for load in first_loads + loads:
        load.start()

    row16 = iota((16, 256), 0)
    gains = jnp.where(
        row16 == 0,
        gain_expert[0:256].astype(F32).reshape(1, 256),
        jnp.where(
            row16 == 1,
            gain_expert[256:512].astype(F32).reshape(1, 256),
            jnp.where(row16 == 2, gain_amateur[...].astype(F32).reshape(1, 256), 0.0),
        ),
    )
    amateur[c, z, 256:272, :] = gains.astype(BF16)

    row_i, col_i = iota((128, 128), 0), iota((128, 128), 1)
    limit = jnp.zeros((128, 128), jnp.int32)
    for r in range(4):
        limit = jnp.where(row_i // 32 == r, lengths[sec * 4 + r], limit)
    live_old = (row_i // 32 == (col_i // 4) % 4) & (row_i % 32 + mp * 32 < limit)
    row_n, col_n = iota((16, 128), 0), iota((16, 128), 1)
    live_new = (row_n // 4 == (col_n // 4) % 4) & (row_n % 4 <= col_n % 4) & (mp == 0)
    for load in first_loads + loads[0:2]:
        load.wait()

    def stacked(ref, start):
        part = ref[:, :, pl.ds(start, HD)].astype(F32)
        return jnp.concatenate([part[r] for r in range(4)], axis=0)

    def attend(i, carry):
        g = i
        base = pl.multiple_of(g * HD, HD)
        keys_old = keys_v[:, :, pl.ds(base, HD)].reshape(128, HD)
        values_old = values_v[:, :, pl.ds(base, HD)].reshape(128, HD)
        keys_new = stacked(new_keys_v, base).astype(BF16)
        values_new = stacked(new_values_v, base).astype(BF16)
        query = jnp.concatenate(
            [stacked(queries_v, pl.multiple_of(g * 1024 + h * HD, HD)) for h in range(8)], axis=0
        ).astype(BF16)
        scaling = 1.0 / HD**0.5
        s_old = lax.dot_general(keys_old, query, NT, preferred_element_type=F32) * scaling
        s_new = lax.dot_general(keys_new, query, NT, preferred_element_type=F32) * scaling
        s_old = jnp.where(live_old, s_old, NEGATIVE)
        s_new = jnp.where(live_new, s_new, NEGATIVE)
        top = jnp.maximum(
            jnp.max(s_old, axis=0, keepdims=True), jnp.max(s_new, axis=0, keepdims=True)
        )
        top = top.astype(BF16).astype(F32)
        p_old = jnp.where(live_old, jnp.exp(s_old - top), 0.0)
        p_new = jnp.where(live_new, jnp.exp(s_new - top), 0.0)
        total = jnp.sum(p_old, axis=0, keepdims=True) + jnp.sum(p_new, axis=0, keepdims=True)
        mix = lax.dot_general(
            p_old.astype(BF16), values_old, TN, preferred_element_type=F32
        ) + lax.dot_general(p_new.astype(BF16), values_new, TN, preferred_element_type=F32)
        high = total.astype(BF16).astype(F32)
        tile = jnp.where(
            row_n == 0,
            top,
            jnp.where(row_n == 1, high, jnp.where(row_n == 2, total - high, 0.0)),
        ).astype(BF16)
        mix = mix.astype(BF16)
        for e in range(2):
            state_out[2 * g + e, 0:64, :] = mix[e * 64 : e * 64 + 64]
            state_out[2 * g + e, 64:80, :] = tile
        return carry

    lax.fori_loop(0, 8, attend, 0)
    pl.semaphore_wait(barrier, 30)

    def send_state(k, carry):
        dest = far_mp(k)
        rcopy(
            state_out.at[dest], state_in.at[mp], state_sem.at[0], state_sem.at[1], at_mp(dest)
        ).start()
        return carry

    lax.fori_loop(0, 15, send_state, 0)

    def am_copy(way, step):
        if way == 0:
            shard, target = (z - step + 9) % 8, (z + 1) % 8
        else:
            shard, target = (z + step - 1) % 8, (z + 7) % 8
        ref = amateur.at[c, shard]
        return rcopy(ref, ref, am_send.at[way, step], am_recv.at[way, step], at_z(target))

    def am_relay(shard, cc):
        ref = amateur.at[cc, shard]
        return rcopy(ref, ref, am_rsend.at[shard], am_rrecv.at[shard], sibling)

    def am_advance(step):
        am_copy(0, step).wait_recv()
        if step < 4:
            am_copy(1, step).wait_recv()
            am_copy(0, step + 1).start()
            if step < 3:
                am_copy(1, step + 1).start()
            am_relay((z + step) % 8, c).start()
        am_relay((z - step + 8) % 8, c).start()

    am_copy(0, 1).start()
    am_copy(1, 1).start()
    am_relay(z, c).start()
    state_in[mp] = state_out[mp]
    fifteen = pl.ds(0, 15)
    state_all = rcopy(
        state_out.at[fifteen], state_in.at[fifteen], state_sem.at[0], state_sem.at[1], sibling
    )
    state_all.wait_recv()

    tiles = [state_in[k, 64:80, :].astype(F32) for k in range(16)]
    top = tiles[0][0:1]
    for k in range(1, 16):
        top = jnp.maximum(top, tiles[k][0:1])
    total = jnp.zeros((1, 128), F32)
    weights = jnp.zeros((128, 128), F32)
    for k in range(16):
        scale = jnp.exp(tiles[k][0:1] - top)
        total = total + scale * (tiles[k][1:2] + tiles[k][2:3])
        weights = jnp.where(row_i == k, scale, weights)
    scale_t[...] = (weights / total).T
    own = scale_t[pl.ds(pl.multiple_of((mp % 2) * 64, 64), 64), :]
    mixed = jnp.zeros((64, HD), F32)
    for k in range(16):
        mixed = mixed + own[:, k : k + 1] * state_in[k, 0:64, :].astype(F32)

    block = dp * 2 + sec
    attended[block] = mixed.astype(BF16).reshape(4, 16, HD)

    def send_attended(k, carry):
        ref = attended.at[block]
        rcopy(ref, ref, attended_sem.at[0], attended_sem.at[1], at_n(far_n(k))).start()
        return carry

    lax.fori_loop(0, 15, send_attended, 0)
    loads[2].wait()
    loads[5].wait()
    fifteen_a = attended.at[fifteen]
    attended_all = rcopy(fifteen_a, fifteen_a, attended_sem.at[0], attended_sem.at[1], sibling)
    attended_all.wait_recv()
    partial = jnp.zeros((256, 512), F32)
    for h in range(4):
        partial = partial + jnp.dot(
            attended[:, h].reshape(256, HD),
            weight_v[h * HD : (h + 1) * HD, :],
            preferred_element_type=F32,
        )
    part_out[...] = partial.astype(BF16).reshape(16, 16, 512)

    def send_part(k, carry):
        dest = far_mp(k)
        rcopy(
            part_out.at[dest], part_in.at[mp], part_sem.at[0], part_sem.at[1], at_mp(dest)
        ).start()
        return carry

    lax.fori_loop(0, 15, send_part, 0)
    part_in[mp] = part_out[mp]
    am_advance(1)
    part_all = rcopy(
        part_in.at[fifteen], part_in.at[fifteen], part_sem.at[0], part_sem.at[1], sibling
    )
    part_all.wait_recv()
    hidden = resid_v[...].astype(F32)
    projected = part_in[0].astype(F32)
    for k in range(1, 16):
        projected = projected + part_in[k].astype(F32)
    full[c, 3, v, u] = (hidden + projected).astype(BF16)

    def one(slot, target):
        return rcopy(
            full.at[c, 3, v, u], full.at[c, slot, v, u], one_send, one_recv.at[slot], at_z(target)
        )

    def send_one(k, carry):
        one((11 - hop(k)) % 8, (z + hop(k)) % 8).start()
        return carry

    lax.fori_loop(0, 7, send_one, 0)

    def two(half, k):
        ref = full.at[c, pl.ds(half * 4, 4), v, u]
        return rcopy(
            ref, ref, two_send.at[half], two_recv.at[half], at_uv((u + k) % 4, v)
        )

    def three(k, zz, vv):
        ref = full.at[c, zz, vv]
        return rcopy(
            ref, ref, three_send.at[zz], three_recv.at[k, zz], at_uv(u, (v + k) % 4)
        )

    def relay(zz, cc):
        ref = full.at[cc, zz]
        return rcopy(ref, ref, relay_send.at[zz], relay_recv.at[zz], sibling)

    for half in range(2):

        def wait_one(zz, carry):
            @pl.when(zz != 3)
            def _():
                one(zz, z).wait_recv()

            return carry

        lax.fori_loop(half * 4, half * 4 + 4, wait_one, 0)
        for k in range(1, 4):
            two(half, k).start()

    am_advance(2)

    def two_all(half):
        ref = full.at[c, pl.ds(half * 4, 4), v, pl.ds(0, 3)]
        return rcopy(ref, ref, two_send.at[half], two_recv.at[half], sibling)

    def send_three(zz, carry):
        for k in (2, 1, 3):
            three(k, zz, v).start()
        return carry

    two_all(0).wait_recv()
    lax.fori_loop(0, 4, send_three, 0)
    am_advance(3)

    loads[3].wait()
    acc_a[...] = jnp.zeros_like(acc_a)
    acc_e[...] = jnp.zeros_like(acc_e)
    square_a[...] = jnp.zeros_like(square_a)
    square_e[...] = jnp.zeros_like(square_e)

    def am_block(j, carry):
        k = (z + 5 + j) % 8
        am_relay(k, 1 - c).wait_recv()
        parts = []
        squares = square_a[...]
        for cc in range(2):
            wide = amateur[cc, k, 0:256, :].astype(F32)
            gain = amateur[cc, k, 256:272, :].astype(F32)[2:3]
            squares = squares + wide[:, 0:128] * wide[:, 0:128] + wide[:, 128:] * wide[:, 128:]
            parts.append((wide * gain).astype(BF16))
        square_a[...] = squares
        acc_a[...] += lax.dot_general(
            ha_v[:, pl.ds(pl.multiple_of(k * 512, 512), 512)],
            jnp.concatenate(parts, axis=1),
            NT,
            preferred_element_type=F32,
        )
        return carry

    lax.fori_loop(0, 7, am_block, 0)
    ones = jnp.ones((8, 128), F32)

    def inverse_norm(ref, width):
        sums = lax.dot_general(
            ones, ref[...], NT, preferred_element_type=F32, precision=lax.Precision.HIGHEST
        )
        return lax.rsqrt(sums[0:1] / width + EPSILON)

    row8 = iota((8, 128), 0)

    def pack(rows):
        tile = jnp.zeros((8, 128), F32)
        for k, row in enumerate(rows):
            tile = jnp.where(row8 == k, row, tile)
        return tile

    def halves(rows):
        return pack([row[:, h * 128 : h * 128 + 128] for row in rows for h in range(2)])

    def join(tiles):
        top = tiles[0]
        for tile in tiles[1:]:
            top = jnp.maximum(top, tile)
        top = top[0:2]
        total, pick = jnp.zeros((2, 128), F32), jnp.zeros((2, 128), F32)
        for tile in tiles:
            total = total + tile[2:4] * jnp.exp(tile[0:2] - top)
            pick = pick + tile[4:6]
        return top, total, pick

    def joined(tiles):
        return pack([part[h : h + 1] for part in join(tiles) for h in range(2)])

    fifteen_p = stats_p.at[0, fifteen]
    seven_z = stats_z.at[0, pl.ds(0, 7)]

    def pair(which):
        return rcopy(
            stats_s.at[which, 0],
            stats_s.at[which, 1],
            stats_send.at[which, 0],
            stats_recv.at[which, 0],
            sibling,
        )

    def start_pair(which, rows):
        stats_s[which, 0] = halves(rows)
        pair(which).start()

    def start_p(which):
        pair(which).wait_recv()
        stats_p[which, mp] = joined([stats_s[which, 0], stats_s[which, 1]])

        def send_p(k, carry):
            ref = stats_p.at[which, mp]
            rcopy(
                ref, ref, stats_send.at[which, 1], stats_recv.at[which, 1], at_mp(far_mp(k))
            ).start()
            return carry

        lax.fori_loop(0, 15, send_p, 0)

    def p_all(which):
        return rcopy(
            fifteen_p, fifteen_p, stats_send.at[which, 1], stats_recv.at[which, 1], sibling
        )

    def start_z(which):
        p_all(which).wait_recv()
        stats_z[which, z] = joined([stats_p[which, k] for k in range(16)])

        def send_z(k, carry):
            ref = stats_z.at[which, z]
            rcopy(
                ref, ref, stats_send.at[which, 2], stats_recv.at[which, 2], at_z((z + hop(k)) % 8)
            ).start()
            return carry

        lax.fori_loop(0, 7, send_z, 0)

    def z_all(which):
        return rcopy(seven_z, seven_z, stats_send.at[which, 2], stats_recv.at[which, 2], sibling)

    def settle(which):
        pair(which).wait_send()
        p_all(which).wait_send()
        z_all(which).wait_send()

    two_all(1).wait_recv()
    loads[4].wait()

    def gather_block(zz, carry):
        @pl.when(zz < 8)
        def _():
            for k in (1, 3, 2):
                three(k, zz, (v - k + 4) % 4).wait_recv()
            relay(zz, c).start()

            @pl.when(zz < 4)
            def _():
                send_three(zz + 4, 0)


        @pl.when(zz >= 1)
        def _():
            k = zz - 1
            relay(k, 1 - c).wait_recv()
            parts = []
            squares = square_e[...]
            for cc in range(2):
                wide = full[cc, k]
                if cc == 0:
                    wide = jnp.swapaxes(wide, 0, 1)
                wide = wide.reshape(256, 512).astype(F32)
                tile = amateur[cc, (z + 5 + k) % 8, 256:272, :].astype(F32)
                for half in range(2):
                    piece = wide[:, half * 256 : half * 256 + 256]
                    squares = (
                        squares
                        + piece[:, 0:128] * piece[:, 0:128]
                        + piece[:, 128:] * piece[:, 128:]
                    )
                    parts.append((piece * tile[half : half + 1]).astype(BF16))
            square_e[...] = squares
            acc_e[...] += lax.dot_general(
                he_v[:, pl.ds(pl.multiple_of((z + 5 + k) % 8 * 1024, 1024), 1024)],
                jnp.concatenate(parts, axis=1),
                NT,
                preferred_element_type=F32,
            )

        return carry

    lax.fori_loop(0, 3, gather_block, 0)
    am_advance(4)
    lax.fori_loop(3, 4, gather_block, 0)
    lax.fori_loop(7, 8, am_block, 0)
    logits_a = acc_a[...] * inverse_norm(square_a, 4096.0)
    acc_a[...] = logits_a
    top_a = jnp.max(logits_a, axis=0, keepdims=True)
    total_a = jnp.sum(jnp.exp(logits_a - top_a), axis=0, keepdims=True)
    start_pair(1, (top_a, total_a))
    lax.fori_loop(4, 6, gather_block, 0)
    start_p(1)
    lax.fori_loop(6, 9, gather_block, 0)

    logits_e = acc_e[...] * inverse_norm(square_e, 8192.0)
    top_e = jnp.max(logits_e, axis=0, keepdims=True)
    total_e = jnp.sum(jnp.exp(logits_e - top_e), axis=0, keepdims=True)
    difference = logits_e - CONTRAST * acc_a[...]
    pick_row = (iota((64, 256), 1) // 4 == iota((64, 256), 0)).astype(F32)
    step_row = iota((8, 256), 1) % 4 == iota((8, 256), 0)
    spread = jnp.dot(
        chosen[...].astype(F32),
        pick_row,
        preferred_element_type=F32,
        precision=lax.Precision.HIGHEST,
    )
    target = jnp.sum(jnp.where(step_row[0:4], spread, 0.0), axis=0, keepdims=True)
    target = target - ((n * 16 + mp) * 512).astype(F32)
    matched = iota((512, 256), 0).astype(F32) == target
    picked = jnp.sum(jnp.where(matched, difference, 0.0), axis=0, keepdims=True)

    start_pair(0, (top_e, total_e, picked))
    start_p(0)
    start_z(1)
    diff[...] = difference.T

    state_all.wait_send()
    attended_all.wait_send()
    for step in range(1, 5):
        am_copy(0, step).wait_send()
        if step < 4:
            am_copy(1, step).wait_send()
    part_all.wait_send()
    ref = full.at[c, pl.ds(0, 7), v, u]
    rcopy(ref, ref, one_send, one_recv.at[0], sibling).wait_send()
    for half in range(2):
        two_all(half).wait_send()

    def drain(k, carry):
        relay(k, c).wait_send()
        am_relay(k, c).wait_send()
        ref = full.at[c, k, pl.ds(0, 3)]
        rcopy(ref, ref, three_send.at[k], three_recv.at[1, k], sibling).wait_send()
        return carry

    lax.fori_loop(0, 8, drain, 0)
    start_z(0)
    settle(1)
    z_all(1).wait_recv()
    top, total, _ = join([stats_z[1, k] for k in range(8)])
    lse_a = top + jnp.log(total)
    z_all(0).wait_recv()
    top, total, pick = join([stats_z[0, k] for k in range(8)])
    shift = top + jnp.log(total) - CONTRAST * lse_a
    chosen_row = pick - shift
    shift = jnp.concatenate([shift[0:1], shift[1:2]], axis=1)
    chosen_row = jnp.concatenate([chosen_row[0:1], chosen_row[1:2]], axis=1)
    shift_t = jnp.broadcast_to(shift, (128, 256)).T
    out[...] = (diff[...] - shift_t[:, 0:1]).reshape(64, 4, 512).astype(BF16)
    masked = jnp.where(step_row, chosen_row, 0.0)
    out_chosen[...] = lax.dot_general(
        masked, pick_row, NT, preferred_element_type=F32, precision=lax.Precision.HIGHEST
    )[0:4]
    settle(0)


def finish(scores, chosen_score, out, out_chosen):
    out[...] = scores[...]
    out_chosen[...] = chosen_score[...]


def local(
    queries,
    new_keys,
    new_values,
    cache_keys,
    cache_values,
    lengths,
    out_weight,
    resid_expert,
    gain_expert,
    hidden_amateur,
    gain_amateur,
    head_expert,
    head_amateur,
    chosen,
):
    vmem = pl.BlockSpec(memory_space=pltpu.VMEM)
    hbm = pl.BlockSpec(memory_space=pl.ANY)
    dma = pltpu.SemaphoreType.DMA
    scores, chosen_score = pl.pallas_call(
        kernel,
        out_shape=(
            jax.ShapeDtypeStruct((64, 4, 512), BF16),
            jax.ShapeDtypeStruct((4, 64), F32),
        ),
        in_specs=[pl.BlockSpec(memory_space=pltpu.SMEM)]
        + [hbm] * 4
        + [vmem] * 2
        + [hbm]
        + [vmem]
        + [hbm] * 5,
        out_specs=(vmem, vmem),
        scratch_shapes=[
            pltpu.VMEM((4, 4, 8192), BF16),
            pltpu.VMEM((4, 4, 1024), BF16),
            pltpu.VMEM((4, 4, 1024), BF16),
            pltpu.VMEM((16, 512), BF16),
            pltpu.VMEM((4, 32, 1024), BF16),
            pltpu.VMEM((4, 32, 1024), BF16),
            pltpu.VMEM((512, 512), BF16),
            pltpu.VMEM((512, 8192), BF16),
            pltpu.VMEM((512, 4096), BF16),
            pltpu.VMEM((16, 80, 128), BF16),
            pltpu.VMEM((16, 80, 128), BF16),
            pltpu.VMEM((128, 128), F32),
            pltpu.VMEM((16, 4, 16, 128), BF16),
            pltpu.VMEM((16, 16, 512), BF16),
            pltpu.VMEM((16, 16, 512), BF16),
            pltpu.VMEM((2, 8, 4, 4, 16, 512), BF16),
            pltpu.VMEM((2, 8, 272, 256), BF16),
            pltpu.VMEM((512, 256), F32),
            pltpu.VMEM((512, 256), F32),
            pltpu.VMEM((256, 128), F32),
            pltpu.VMEM((256, 128), F32),
            pltpu.VMEM((256, 512), F32),
            pltpu.VMEM((2, 2, 8, 128), F32),
            pltpu.VMEM((2, 16, 8, 128), F32),
            pltpu.VMEM((2, 8, 8, 128), F32),
            dma((10,)),
            dma((2,)),
            dma((2,)),
            dma((2,)),
            dma,
            dma((8,)),
            dma((2,)),
            dma((2,)),
            dma((8,)),
            dma((4, 8)),
            dma((8,)),
            dma((8,)),
            dma((2, 5)),
            dma((2, 5)),
            dma((8,)),
            dma((8,)),
            dma((2, 3)),
            dma((2, 3)),
        ],
        compiler_params=pltpu.CompilerParams(
            collective_id=0, has_side_effects=True, vmem_limit_bytes=56 * 1024 * 1024
        ),
        name="contrast",
    )(
        lengths,
        queries,
        new_keys,
        new_values,
        resid_expert,
        gain_expert,
        gain_amateur,
        hidden_amateur,
        chosen.T,
        cache_keys,
        cache_values,
        out_weight,
        head_expert,
        head_amateur,
    )
    scores, chosen_score = pl.pallas_call(
        finish,
        out_shape=(
            jax.ShapeDtypeStruct((64, 4, 512), BF16),
            jax.ShapeDtypeStruct((4, 64), F32),
        ),
        in_specs=[vmem] * 2,
        out_specs=(vmem, vmem),
        name="finish",
    )(scores, chosen_score)
    return scores, chosen_score.T


def solution(mesh):
    return jax.shard_map(
        local,
        mesh=mesh,
        in_specs=(
            P("dp", None, None),
            P("dp", None, None),
            P("dp", None, None),
            P("dp", "mp", None),
            P("dp", "mp", None),
            P("dp"),
            P("mp", ("section", "dp")),
            P(None, ("section", "dp")),
            P(("section", "dp")),
            P(None, ("section", "dp")),
            P(("section", "dp")),
            P(("section", "dp", "mp"), None),
            P(("section", "dp", "mp"), None),
            P(),
        ),
        out_specs=(P(None, None, ("section", "dp", "mp")), P()),
        check_vma=False,
    )
```

```python
import jax
import jax.numpy as jnp
from jax import lax
from jax.experimental import pallas as pl
from jax.experimental.pallas import tpu as pltpu
from jax.sharding import PartitionSpec as P

MESH = pl.DeviceIdType.MESH
F32 = jnp.float32
BF16 = jnp.bfloat16
KVH = 8
HD = 128
CONTRAST = 0.5
NEGATIVE = -1e30
EPSILON = 1e-05
NT = (((1,), (1,)), ((), ()))
TN = (((0,), (0,)), ((), ()))


def rcopy(src, dst, send_sem, recv_sem, device):
    return pltpu.make_async_remote_copy(
        src_ref=src,
        dst_ref=dst,
        send_sem=send_sem,
        recv_sem=recv_sem,
        device_id=device,
        device_id_type=MESH,
    )


def iota(shape, dim):
    return lax.broadcasted_iota(jnp.int32, shape, dim)


def place(i):
    return (2 - i + 3 * (i // 2) + 2 * (i // 3)) % 4


def hop(k):
    return (4 + (k + 1) // 2 * (1 - 2 * (k % 2))) % 8


def kernel(
    lengths,
    queries,
    new_keys,
    new_values,
    resid,
    gain_expert,
    gain_amateur,
    hidden_amateur,
    chosen,
    cache_keys,
    cache_values,
    out_weight,
    head_expert,
    head_amateur,
    out_diff,
    out_rows,
    queries_v,
    new_keys_v,
    new_values_v,
    resid_v,
    keys_v,
    values_v,
    weight_v,
    he_v,
    ha_v,
    state_out,
    state_in,
    scale_t,
    attended,
    part_out,
    part_in,
    full,
    amateur,
    acc_e,
    acc_a,
    square_e,
    square_a,
    diff,
    target_v,
    stats_s,
    stats_p,
    stats_z,
    load_sem,
    state_sem,
    attended_sem,
    part_sem,
    one_send,
    one_recv,
    two_send,
    two_recv,
    three_send,
    three_recv,
    relay_send,
    relay_recv,
    am_send,
    am_recv,
    am_rsend,
    am_rrecv,
    stats_send,
    stats_recv,
):
    sec = lax.axis_index("section")
    dp = lax.axis_index("dp")
    mp = lax.axis_index("mp")
    z = sec * 4 + dp // 2
    c = dp % 2
    n = sec * 8 + dp
    x, y = mp // 4, mp % 4
    u = x * (1 - c) + y * c
    v = y * (1 - c) + x * c

    def at_n(k):
        return (k // 8, k % 8, mp)

    def at_z(zz):
        return (zz // 4, (zz % 4) * 2 + c, mp)

    def at_mp(k):
        return (sec, dp, k)

    def at_uv(uu, vv):
        return (sec, dp, (uu * 4 + vv) * (1 - c) + (vv * 4 + uu) * c)

    def far_mp(k):
        return (x + place(k % 4)) % 4 * 4 + (y + place(k // 4)) % 4

    def far_n(k):
        return (z + hop(k // 2)) % 8 * 2 + (c + 1 + k) % 2

    sibling = (sec, dp + 1 - 2 * c, mp)

    mine = pl.ds(sec * 4, 4)
    loads = [
        pltpu.make_async_copy(cache_keys.at[pl.ds(sec * 4, 4)], keys_v, load_sem.at[0]),
        pltpu.make_async_copy(cache_values.at[pl.ds(sec * 4, 4)], values_v, load_sem.at[1]),
        pltpu.make_async_copy(out_weight, weight_v, load_sem.at[2]),
        pltpu.make_async_copy(head_amateur, ha_v, load_sem.at[3]),
        pltpu.make_async_copy(head_expert, he_v, load_sem.at[4]),
        pltpu.make_async_copy(
            resid.at[pl.ds(pl.multiple_of(mp * 16, 16), 16)], resid_v, load_sem.at[5]
        ),
    ]
    first_loads = [
        pltpu.make_async_copy(queries.at[mine], queries_v, load_sem.at[6]),
        pltpu.make_async_copy(new_keys.at[mine], new_keys_v, load_sem.at[7]),
        pltpu.make_async_copy(new_values.at[mine], new_values_v, load_sem.at[8]),
        pltpu.make_async_copy(hidden_amateur, amateur.at[c, z, pl.ds(0, 256)], load_sem.at[9]),
    ]

    barrier = pltpu.get_barrier_semaphore()

    def greet_mp(k, carry):
        pl.semaphore_signal(
            barrier, inc=1, device_id=at_mp(far_mp(k)), device_id_type=MESH
        )
        return carry

    def greet_n(k, carry):
        pl.semaphore_signal(
            barrier, inc=1, device_id=at_n(far_n(k)), device_id_type=MESH
        )
        return carry

    lax.fori_loop(0, 15, greet_n, 0)
    lax.fori_loop(0, 15, greet_mp, 0)
    for load in first_loads + loads:
        load.start()

    row16 = iota((16, 256), 0)
    gains = jnp.where(
        row16 == 0,
        gain_expert[0:256].astype(F32).reshape(1, 256),
        jnp.where(
            row16 == 1,
            gain_expert[256:512].astype(F32).reshape(1, 256),
            jnp.where(row16 == 2, gain_amateur[...].astype(F32).reshape(1, 256), 0.0),
        ),
    )
    amateur[c, z, 256:272, :] = gains.astype(BF16)

    pick_row = (iota((64, 256), 1) // 4 == iota((64, 256), 0)).astype(F32)
    step_row = iota((8, 256), 1) % 4 == iota((8, 256), 0)
    spread = jnp.dot(
        chosen[...].astype(F32),
        pick_row,
        preferred_element_type=F32,
        precision=lax.Precision.HIGHEST,
    )
    target = jnp.sum(jnp.where(step_row[0:4], spread, 0.0), axis=0, keepdims=True)
    target = target - ((n * 16 + mp) * 512).astype(F32)
    target_v[...] = jnp.broadcast_to(target, (8, 256))

    row_i, col_i = iota((128, 128), 0), iota((128, 128), 1)
    limit = jnp.zeros((128, 128), jnp.int32)
    for r in range(4):
        limit = jnp.where(row_i // 32 == r, lengths[sec * 4 + r], limit)
    live_old = (row_i // 32 == (col_i // 4) % 4) & (row_i % 32 + mp * 32 < limit)
    row_n, col_n = iota((16, 128), 0), iota((16, 128), 1)
    live_new = (row_n // 4 == (col_n // 4) % 4) & (row_n % 4 <= col_n % 4) & (mp == 0)
    for load in first_loads + loads[0:2]:
        load.wait()

    def stacked(ref, start):
        part = ref[:, :, pl.ds(start, HD)].astype(F32)
        return jnp.concatenate([part[r] for r in range(4)], axis=0)

    def attend(i, carry):
        g = i
        base = pl.multiple_of(g * HD, HD)
        keys_old = keys_v[:, :, pl.ds(base, HD)].reshape(128, HD)
        values_old = values_v[:, :, pl.ds(base, HD)].reshape(128, HD)
        keys_new = stacked(new_keys_v, base).astype(BF16)
        values_new = stacked(new_values_v, base).astype(BF16)
        query = jnp.concatenate(
            [stacked(queries_v, pl.multiple_of(g * 1024 + h * HD, HD)) for h in range(8)], axis=0
        ).astype(BF16)
        scaling = 1.0 / HD**0.5
        s_old = lax.dot_general(keys_old, query, NT, preferred_element_type=F32) * scaling
        s_new = lax.dot_general(keys_new, query, NT, preferred_element_type=F32) * scaling
        s_old = jnp.where(live_old, s_old, NEGATIVE)
        s_new = jnp.where(live_new, s_new, NEGATIVE)
        top = jnp.maximum(
            jnp.max(s_old, axis=0, keepdims=True), jnp.max(s_new, axis=0, keepdims=True)
        )
        top = top.astype(BF16).astype(F32)
        p_old = jnp.where(live_old, jnp.exp(s_old - top), 0.0)
        p_new = jnp.where(live_new, jnp.exp(s_new - top), 0.0)
        total = jnp.sum(p_old, axis=0, keepdims=True) + jnp.sum(p_new, axis=0, keepdims=True)
        mix = lax.dot_general(
            p_old.astype(BF16), values_old, TN, preferred_element_type=F32
        ) + lax.dot_general(p_new.astype(BF16), values_new, TN, preferred_element_type=F32)
        high = total.astype(BF16).astype(F32)
        tile = jnp.where(
            row_n == 0,
            top,
            jnp.where(row_n == 1, high, jnp.where(row_n == 2, total - high, 0.0)),
        ).astype(BF16)
        mix = mix.astype(BF16)
        for e in range(2):
            state_out[2 * g + e, 0:64, :] = mix[e * 64 : e * 64 + 64]
            state_out[2 * g + e, 64:80, :] = tile
        return carry

    lax.fori_loop(0, 8, attend, 0)
    pl.semaphore_wait(barrier, 30)

    def send_state(k, carry):
        dest = far_mp(k)
        rcopy(
            state_out.at[dest], state_in.at[mp], state_sem.at[0], state_sem.at[1], at_mp(dest)
        ).start()
        return carry

    lax.fori_loop(0, 15, send_state, 0)

    def am_copy(way, step):
        if way == 0:
            shard, target = (z - step + 9) % 8, (z + 1) % 8
        else:
            shard, target = (z + step - 1) % 8, (z + 7) % 8
        ref = amateur.at[c, shard]
        return rcopy(ref, ref, am_send.at[way, step], am_recv.at[way, step], at_z(target))

    def am_relay(shard, cc):
        ref = amateur.at[cc, shard]
        return rcopy(ref, ref, am_rsend.at[shard], am_rrecv.at[shard], sibling)

    def am_advance(step):
        am_copy(0, step).wait_recv()
        if step < 4:
            am_copy(1, step).wait_recv()
            am_copy(0, step + 1).start()
            if step < 3:
                am_copy(1, step + 1).start()
            am_relay((z + step) % 8, c).start()
        am_relay((z - step + 8) % 8, c).start()

    am_copy(0, 1).start()
    am_copy(1, 1).start()
    am_relay(z, c).start()
    state_in[mp] = state_out[mp]
    fifteen = pl.ds(0, 15)
    state_all = rcopy(
        state_out.at[fifteen], state_in.at[fifteen], state_sem.at[0], state_sem.at[1], sibling
    )
    state_all.wait_recv()

    tiles = [state_in[k, 64:80, :].astype(F32) for k in range(16)]
    top = tiles[0][0:1]
    for k in range(1, 16):
        top = jnp.maximum(top, tiles[k][0:1])
    total = jnp.zeros((1, 128), F32)
    weights = jnp.zeros((128, 128), F32)
    for k in range(16):
        scale = jnp.exp(tiles[k][0:1] - top)
        total = total + scale * (tiles[k][1:2] + tiles[k][2:3])
        weights = jnp.where(row_i == k, scale, weights)
    scale_t[...] = (weights / total).T
    own = scale_t[pl.ds(pl.multiple_of((mp % 2) * 64, 64), 64), :]
    mixed = jnp.zeros((64, HD), F32)
    for k in range(16):
        mixed = mixed + own[:, k : k + 1] * state_in[k, 0:64, :].astype(F32)

    block = dp * 2 + sec
    attended[block] = mixed.astype(BF16).reshape(4, 16, HD)

    def send_attended(k, carry):
        ref = attended.at[block]
        rcopy(ref, ref, attended_sem.at[0], attended_sem.at[1], at_n(far_n(k))).start()
        return carry

    lax.fori_loop(0, 15, send_attended, 0)
    loads[2].wait()
    loads[5].wait()
    fifteen_a = attended.at[fifteen]
    attended_all = rcopy(fifteen_a, fifteen_a, attended_sem.at[0], attended_sem.at[1], sibling)
    attended_all.wait_recv()
    partial = jnp.zeros((256, 512), F32)
    for h in range(4):
        partial = partial + jnp.dot(
            attended[:, h].reshape(256, HD),
            weight_v[h * HD : (h + 1) * HD, :],
            preferred_element_type=F32,
        )
    part_out[...] = partial.astype(BF16).reshape(16, 16, 512)

    def send_part(k, carry):
        dest = far_mp(k)
        rcopy(
            part_out.at[dest], part_in.at[mp], part_sem.at[0], part_sem.at[1], at_mp(dest)
        ).start()
        return carry

    lax.fori_loop(0, 15, send_part, 0)
    part_in[mp] = part_out[mp]
    am_advance(1)
    part_all = rcopy(
        part_in.at[fifteen], part_in.at[fifteen], part_sem.at[0], part_sem.at[1], sibling
    )
    part_all.wait_recv()
    hidden = resid_v[...].astype(F32)
    projected = part_in[0].astype(F32)
    for k in range(1, 16):
        projected = projected + part_in[k].astype(F32)
    full[c, 3, v, u] = (hidden + projected).astype(BF16)

    def one(slot, target):
        return rcopy(
            full.at[c, 3, v, u], full.at[c, slot, v, u], one_send, one_recv.at[slot], at_z(target)
        )

    def send_one(k, carry):
        one((11 - hop(k)) % 8, (z + hop(k)) % 8).start()
        return carry

    lax.fori_loop(0, 7, send_one, 0)

    def two(half, k):
        ref = full.at[c, pl.ds(half * 2, 2), v, u]
        return rcopy(
            ref, ref, two_send.at[half], two_recv.at[half], at_uv((u + k) % 4, v)
        )

    def three(k, zz, vv):
        ref = full.at[c, zz, vv]
        return rcopy(
            ref, ref, three_send.at[zz], three_recv.at[k, zz], at_uv(u, (v + k) % 4)
        )

    def relay(zz, cc):
        ref = full.at[cc, zz]
        return rcopy(ref, ref, relay_send.at[zz], relay_recv.at[zz], sibling)

    for half in range(4):

        def wait_one(zz, carry):
            @pl.when(zz != 3)
            def _():
                one(zz, z).wait_recv()

            return carry

        lax.fori_loop(half * 2, half * 2 + 2, wait_one, 0)
        for k in range(1, 4):
            two(half, k).start()

    am_advance(2)

    def two_all(half):
        ref = full.at[c, pl.ds(half * 2, 2), v, pl.ds(0, 3)]
        return rcopy(ref, ref, two_send.at[half], two_recv.at[half], sibling)

    def send_three(zz, carry):
        for k in (2, 1, 3):
            three(k, zz, v).start()
        return carry

    for half in range(2):
        two_all(half).wait_recv()
        lax.fori_loop(half * 2, half * 2 + 2, send_three, 0)
    am_advance(3)

    loads[3].wait()
    acc_a[...] = jnp.zeros_like(acc_a)
    acc_e[...] = jnp.zeros_like(acc_e)
    square_a[...] = jnp.zeros_like(square_a)
    square_e[...] = jnp.zeros_like(square_e)

    def am_block(j, carry):
        k = (z + 5 + j) % 8
        am_relay(k, 1 - c).wait_recv()
        parts = []
        squares = square_a[...]
        for cc in range(2):
            wide = amateur[cc, k, 0:256, :].astype(F32)
            gain = amateur[cc, k, 256:272, :].astype(F32)[2:3]
            squares = squares + wide[:, 0:128] * wide[:, 0:128] + wide[:, 128:] * wide[:, 128:]
            parts.append((wide * gain).astype(BF16))
        square_a[...] = squares
        acc_a[...] += lax.dot_general(
            ha_v[:, pl.ds(pl.multiple_of(k * 512, 512), 512)],
            jnp.concatenate(parts, axis=1),
            NT,
            preferred_element_type=F32,
        )
        return carry

    lax.fori_loop(0, 7, am_block, 0)
    ones = jnp.ones((8, 128), F32)

    def chosen_here():
        return iota((512, 256), 0).astype(F32) == target_v[0:1, :]

    def inverse_norm(ref, width):
        sums = lax.dot_general(
            ones, ref[...], NT, preferred_element_type=F32, precision=lax.Precision.HIGHEST
        )
        return lax.rsqrt(sums[0:1] / width + EPSILON)

    row8 = iota((8, 128), 0)

    def pack(rows):
        tile = jnp.zeros((8, 128), F32)
        for k, row in enumerate(rows):
            tile = jnp.where(row8 == k, row, tile)
        return tile

    def halves(rows):
        return pack([row[:, h * 128 : h * 128 + 128] for row in rows for h in range(2)])

    def join(tiles):
        top = tiles[0]
        for tile in tiles[1:]:
            top = jnp.maximum(top, tile)
        top = top[0:2]
        total, pick = jnp.zeros((2, 128), F32), jnp.zeros((2, 128), F32)
        for tile in tiles:
            total = total + tile[2:4] * jnp.exp(tile[0:2] - top)
            pick = pick + tile[4:6]
        return top, total, pick

    def joined(tiles):
        return pack([part[h : h + 1] for part in join(tiles) for h in range(2)])

    fifteen_p = stats_p.at[0, fifteen]
    seven_z = stats_z.at[0, pl.ds(0, 7)]

    def pair(which):
        return rcopy(
            stats_s.at[which, 0],
            stats_s.at[which, 1],
            stats_send.at[which, 0],
            stats_recv.at[which, 0],
            sibling,
        )

    def start_pair(which, rows):
        stats_s[which, 0] = halves(rows)
        pair(which).start()

    def start_p(which):
        pair(which).wait_recv()
        stats_p[which, mp] = joined([stats_s[which, 0], stats_s[which, 1]])

        def send_p(k, carry):
            ref = stats_p.at[which, mp]
            rcopy(
                ref, ref, stats_send.at[which, 1], stats_recv.at[which, 1], at_mp(far_mp(k))
            ).start()
            return carry

        lax.fori_loop(0, 15, send_p, 0)

    def p_all(which):
        return rcopy(
            fifteen_p, fifteen_p, stats_send.at[which, 1], stats_recv.at[which, 1], sibling
        )

    def start_z(which):
        p_all(which).wait_recv()
        stats_z[which, z] = joined([stats_p[which, k] for k in range(16)])

        def send_z(k, carry):
            ref = stats_z.at[which, z]
            rcopy(
                ref, ref, stats_send.at[which, 2], stats_recv.at[which, 2], at_z((z + hop(k)) % 8)
            ).start()
            return carry

        lax.fori_loop(0, 7, send_z, 0)

    def z_all(which):
        return rcopy(seven_z, seven_z, stats_send.at[which, 2], stats_recv.at[which, 2], sibling)

    def settle(which):
        pair(which).wait_send()
        p_all(which).wait_send()
        z_all(which).wait_send()

    two_all(2).wait_recv()
    two_all(3).wait_recv()
    loads[4].wait()

    def gather_block(zz, carry):
        @pl.when(zz < 8)
        def _():
            for k in (1, 3, 2):
                three(k, zz, (v - k + 4) % 4).wait_recv()
            relay(zz, c).start()

            @pl.when(zz < 4)
            def _():
                send_three(zz + 4, 0)


        @pl.when(zz >= 1)
        def _():
            k = zz - 1
            relay(k, 1 - c).wait_recv()
            parts = []
            squares = square_e[...]
            for cc in range(2):
                wide = full[cc, k]
                if cc == 0:
                    wide = jnp.swapaxes(wide, 0, 1)
                wide = wide.reshape(256, 512).astype(F32)
                tile = amateur[cc, (z + 5 + k) % 8, 256:272, :].astype(F32)
                for half in range(2):
                    piece = wide[:, half * 256 : half * 256 + 256]
                    squares = (
                        squares
                        + piece[:, 0:128] * piece[:, 0:128]
                        + piece[:, 128:] * piece[:, 128:]
                    )
                    parts.append((piece * tile[half : half + 1]).astype(BF16))
            square_e[...] = squares
            acc_e[...] += lax.dot_general(
                he_v[:, pl.ds(pl.multiple_of((z + 5 + k) % 8 * 1024, 1024), 1024)],
                jnp.concatenate(parts, axis=1),
                NT,
                preferred_element_type=F32,
            )

        return carry

    lax.fori_loop(0, 3, gather_block, 0)
    am_advance(4)
    lax.fori_loop(3, 4, gather_block, 0)
    lax.fori_loop(7, 8, am_block, 0)
    logits_a = acc_a[...] * inverse_norm(square_a, 4096.0)
    acc_a[...] = logits_a
    top_a = jnp.max(logits_a, axis=0, keepdims=True)
    total_a = jnp.sum(jnp.exp(logits_a - top_a), axis=0, keepdims=True)
    picked_a = jnp.sum(jnp.where(chosen_here(), logits_a, 0.0), axis=0, keepdims=True)
    start_pair(1, (top_a, total_a, picked_a))
    lax.fori_loop(4, 6, gather_block, 0)
    start_p(1)
    lax.fori_loop(6, 9, gather_block, 0)

    logits_e = acc_e[...] * inverse_norm(square_e, 8192.0)
    top_e = jnp.max(logits_e, axis=0, keepdims=True)
    total_e = jnp.sum(jnp.exp(logits_e - top_e), axis=0, keepdims=True)
    picked = jnp.sum(jnp.where(chosen_here(), logits_e, 0.0), axis=0, keepdims=True)

    start_pair(0, (top_e, total_e, picked))
    start_p(0)
    start_z(1)
    diff[...] = (logits_e - CONTRAST * acc_a[...]).T
    store = pltpu.make_async_copy(diff, out_diff, load_sem.at[10])
    store.start()

    state_all.wait_send()
    attended_all.wait_send()
    for step in range(1, 5):
        am_copy(0, step).wait_send()
        if step < 4:
            am_copy(1, step).wait_send()
    part_all.wait_send()
    ref = full.at[c, pl.ds(0, 7), v, u]
    rcopy(ref, ref, one_send, one_recv.at[0], sibling).wait_send()
    for half in range(4):
        two_all(half).wait_send()

    def drain(k, carry):
        relay(k, c).wait_send()
        am_relay(k, c).wait_send()
        ref = full.at[c, k, pl.ds(0, 3)]
        rcopy(ref, ref, three_send.at[k], three_recv.at[1, k], sibling).wait_send()
        return carry

    lax.fori_loop(0, 8, drain, 0)
    start_z(0)
    settle(1)
    z_all(1).wait_recv()
    top, total, pick_a = join([stats_z[1, k] for k in range(8)])
    lse_a = top + jnp.log(total)
    z_all(0).wait_recv()
    top, total, pick = join([stats_z[0, k] for k in range(8)])
    shift = top + jnp.log(total) - CONTRAST * lse_a
    chosen_row = pick - CONTRAST * pick_a - shift
    shift = jnp.concatenate([shift[0:1], shift[1:2]], axis=1)
    chosen_row = jnp.concatenate([chosen_row[0:1], chosen_row[1:2]], axis=1)
    row_8 = iota((8, 256), 0)
    out_rows[...] = jnp.where(row_8 == 0, shift, jnp.where(row_8 == 1, chosen_row, 0.0))
    store.wait()
    settle(0)


def finish(diff, rows, out, out_chosen):
    shift = jnp.broadcast_to(rows[0:1, :], (128, 256)).T
    out[...] = (diff[...] - shift[:, 0:1]).reshape(64, 4, 512).astype(BF16)
    pick_row = (iota((64, 256), 1) // 4 == iota((64, 256), 0)).astype(F32)
    step_row = iota((8, 256), 1) % 4 == iota((8, 256), 0)
    masked = jnp.where(step_row, rows[1:2, :], 0.0)
    out_chosen[...] = lax.dot_general(
        masked, pick_row, NT, preferred_element_type=F32, precision=lax.Precision.HIGHEST
    )[0:4]


def local(
    queries,
    new_keys,
    new_values,
    cache_keys,
    cache_values,
    lengths,
    out_weight,
    resid_expert,
    gain_expert,
    hidden_amateur,
    gain_amateur,
    head_expert,
    head_amateur,
    chosen,
):
    vmem = pl.BlockSpec(memory_space=pltpu.VMEM)
    hbm = pl.BlockSpec(memory_space=pl.ANY)
    dma = pltpu.SemaphoreType.DMA
    diff, rows = pl.pallas_call(
        kernel,
        out_shape=(
            jax.ShapeDtypeStruct((256, 512), F32),
            jax.ShapeDtypeStruct((8, 256), F32),
        ),
        in_specs=[pl.BlockSpec(memory_space=pltpu.SMEM)]
        + [hbm] * 4
        + [vmem] * 2
        + [hbm]
        + [vmem]
        + [hbm] * 5,
        out_specs=(hbm, vmem),
        scratch_shapes=[
            pltpu.VMEM((4, 4, 8192), BF16),
            pltpu.VMEM((4, 4, 1024), BF16),
            pltpu.VMEM((4, 4, 1024), BF16),
            pltpu.VMEM((16, 512), BF16),
            pltpu.VMEM((4, 32, 1024), BF16),
            pltpu.VMEM((4, 32, 1024), BF16),
            pltpu.VMEM((512, 512), BF16),
            pltpu.VMEM((512, 8192), BF16),
            pltpu.VMEM((512, 4096), BF16),
            pltpu.VMEM((16, 80, 128), BF16),
            pltpu.VMEM((16, 80, 128), BF16),
            pltpu.VMEM((128, 128), F32),
            pltpu.VMEM((16, 4, 16, 128), BF16),
            pltpu.VMEM((16, 16, 512), BF16),
            pltpu.VMEM((16, 16, 512), BF16),
            pltpu.VMEM((2, 8, 4, 4, 16, 512), BF16),
            pltpu.VMEM((2, 8, 272, 256), BF16),
            pltpu.VMEM((512, 256), F32),
            pltpu.VMEM((512, 256), F32),
            pltpu.VMEM((256, 128), F32),
            pltpu.VMEM((256, 128), F32),
            pltpu.VMEM((256, 512), F32),
            pltpu.VMEM((8, 256), F32),
            pltpu.VMEM((2, 2, 8, 128), F32),
            pltpu.VMEM((2, 16, 8, 128), F32),
            pltpu.VMEM((2, 8, 8, 128), F32),
            dma((11,)),
            dma((2,)),
            dma((2,)),
            dma((2,)),
            dma,
            dma((8,)),
            dma((4,)),
            dma((4,)),
            dma((8,)),
            dma((4, 8)),
            dma((8,)),
            dma((8,)),
            dma((2, 5)),
            dma((2, 5)),
            dma((8,)),
            dma((8,)),
            dma((2, 3)),
            dma((2, 3)),
        ],
        compiler_params=pltpu.CompilerParams(
            collective_id=0, has_side_effects=True, vmem_limit_bytes=56 * 1024 * 1024
        ),
        name="contrast",
    )(
        lengths,
        queries,
        new_keys,
        new_values,
        resid_expert,
        gain_expert,
        gain_amateur,
        hidden_amateur,
        chosen.T,
        cache_keys,
        cache_values,
        out_weight,
        head_expert,
        head_amateur,
    )
    scores, chosen_score = pl.pallas_call(
        finish,
        out_shape=(
            jax.ShapeDtypeStruct((64, 4, 512), BF16),
            jax.ShapeDtypeStruct((4, 64), F32),
        ),
        in_specs=[vmem] * 2,
        out_specs=(vmem, vmem),
        name="finish",
    )(diff, rows)
    return scores, chosen_score.T


def solution(mesh):
    return jax.shard_map(
        local,
        mesh=mesh,
        in_specs=(
            P("dp", None, None),
            P("dp", None, None),
            P("dp", None, None),
            P("dp", "mp", None),
            P("dp", "mp", None),
            P("dp"),
            P("mp", ("section", "dp")),
            P(None, ("section", "dp")),
            P(("section", "dp")),
            P(None, ("section", "dp")),
            P(("section", "dp")),
            P(("section", "dp", "mp"), None),
            P(("section", "dp", "mp"), None),
            P(),
        ),
        out_specs=(P(None, None, ("section", "dp", "mp")), P()),
        check_vma=False,
    )
```

```python
import jax
import jax.numpy as jnp
from jax import lax
from jax.experimental import pallas as pl
from jax.experimental.pallas import tpu as pltpu
from jax.sharding import PartitionSpec as P

MESH = pl.DeviceIdType.MESH
F32 = jnp.float32
BF16 = jnp.bfloat16
KVH = 8
HD = 128
CONTRAST = 0.5
NEGATIVE = -1e30
EPSILON = 1e-05
NT = (((1,), (1,)), ((), ()))
TN = (((0,), (0,)), ((), ()))


def rcopy(src, dst, send_sem, recv_sem, device):
    return pltpu.make_async_remote_copy(
        src_ref=src,
        dst_ref=dst,
        send_sem=send_sem,
        recv_sem=recv_sem,
        device_id=device,
        device_id_type=MESH,
    )


def iota(shape, dim):
    return lax.broadcasted_iota(jnp.int32, shape, dim)


def place(i):
    return (2 - i + 3 * (i // 2) + 2 * (i // 3)) % 4


def hop(k):
    return (4 + (k + 1) // 2 * (1 - 2 * (k % 2))) % 8


def kernel(
    lengths,
    queries,
    new_keys,
    new_values,
    resid,
    gain_expert,
    gain_amateur,
    hidden_amateur,
    chosen,
    cache_keys,
    cache_values,
    out_weight,
    head_expert,
    head_amateur,
    out_diff,
    out_rows,
    queries_v,
    new_keys_v,
    new_values_v,
    resid_v,
    keys_v,
    values_v,
    weight_v,
    he_v,
    ha_v,
    state_out,
    state_in,
    scale_t,
    attended,
    part_out,
    part_in,
    full,
    amateur,
    acc_e,
    acc_a,
    square_e,
    square_a,
    diff,
    target_v,
    stats_s,
    stats_p,
    stats_z,
    load_sem,
    state_sem,
    attended_sem,
    part_sem,
    one_send,
    one_recv,
    two_send,
    two_recv,
    three_send,
    three_recv,
    relay_send,
    relay_recv,
    am_send,
    am_recv,
    am_rsend,
    am_rrecv,
    stats_send,
    stats_recv,
):
    sec = lax.axis_index("section")
    dp = lax.axis_index("dp")
    mp = lax.axis_index("mp")
    z = sec * 4 + dp // 2
    c = dp % 2
    n = sec * 8 + dp
    x, y = mp // 4, mp % 4
    u = x * (1 - c) + y * c
    v = y * (1 - c) + x * c

    def at_n(k):
        return (k // 8, k % 8, mp)

    def at_z(zz):
        return (zz // 4, (zz % 4) * 2 + c, mp)

    def at_mp(k):
        return (sec, dp, k)

    def at_uv(uu, vv):
        return (sec, dp, (uu * 4 + vv) * (1 - c) + (vv * 4 + uu) * c)

    def far_mp(k):
        return (x + place(k % 4)) % 4 * 4 + (y + place(k // 4)) % 4

    def far_n(k):
        return (z + hop(k // 2)) % 8 * 2 + (c + 1 + k) % 2

    sibling = (sec, dp + 1 - 2 * c, mp)

    mine = pl.ds(sec * 4, 4)
    loads = [
        pltpu.make_async_copy(cache_keys.at[pl.ds(sec * 4, 4)], keys_v, load_sem.at[0]),
        pltpu.make_async_copy(cache_values.at[pl.ds(sec * 4, 4)], values_v, load_sem.at[1]),
        pltpu.make_async_copy(out_weight, weight_v, load_sem.at[2]),
        pltpu.make_async_copy(head_amateur, ha_v, load_sem.at[3]),
        pltpu.make_async_copy(head_expert, he_v, load_sem.at[4]),
        pltpu.make_async_copy(
            resid.at[pl.ds(pl.multiple_of(mp * 16, 16), 16)], resid_v, load_sem.at[5]
        ),
    ]
    first_loads = [
        pltpu.make_async_copy(queries.at[mine], queries_v, load_sem.at[6]),
        pltpu.make_async_copy(new_keys.at[mine], new_keys_v, load_sem.at[7]),
        pltpu.make_async_copy(new_values.at[mine], new_values_v, load_sem.at[8]),
        pltpu.make_async_copy(hidden_amateur, amateur.at[c, z, pl.ds(0, 256)], load_sem.at[9]),
    ]

    barrier = pltpu.get_barrier_semaphore()

    def greet_mp(k, carry):
        pl.semaphore_signal(
            barrier, inc=1, device_id=at_mp(far_mp(k)), device_id_type=MESH
        )
        return carry

    def greet_n(k, carry):
        pl.semaphore_signal(
            barrier, inc=1, device_id=at_n(far_n(k)), device_id_type=MESH
        )
        return carry

    lax.fori_loop(0, 15, greet_n, 0)
    lax.fori_loop(0, 15, greet_mp, 0)
    for load in first_loads + loads:
        load.start()

    row16 = iota((16, 256), 0)
    gains = jnp.where(
        row16 == 0,
        gain_expert[0:256].astype(F32).reshape(1, 256),
        jnp.where(
            row16 == 1,
            gain_expert[256:512].astype(F32).reshape(1, 256),
            jnp.where(row16 == 2, gain_amateur[...].astype(F32).reshape(1, 256), 0.0),
        ),
    )
    amateur[c, z, 256:272, :] = gains.astype(BF16)

    pick_row = (iota((64, 256), 1) // 4 == iota((64, 256), 0)).astype(F32)
    step_row = iota((8, 256), 1) % 4 == iota((8, 256), 0)
    spread = jnp.dot(
        chosen[...].astype(F32),
        pick_row,
        preferred_element_type=F32,
        precision=lax.Precision.HIGHEST,
    )
    target = jnp.sum(jnp.where(step_row[0:4], spread, 0.0), axis=0, keepdims=True)
    target = target - ((n * 16 + mp) * 512).astype(F32)
    target_v[...] = jnp.broadcast_to(target, (8, 256))

    row_i, col_i = iota((128, 128), 0), iota((128, 128), 1)
    limit = jnp.zeros((128, 128), jnp.int32)
    for r in range(4):
        limit = jnp.where(row_i // 32 == r, lengths[sec * 4 + r], limit)
    live_old = (row_i // 32 == (col_i // 4) % 4) & (row_i % 32 + mp * 32 < limit)
    row_n, col_n = iota((16, 128), 0), iota((16, 128), 1)
    live_new = (row_n // 4 == (col_n // 4) % 4) & (row_n % 4 <= col_n % 4) & (mp == 0)
    for load in first_loads + loads[0:2]:
        load.wait()

    def stacked(ref, start):
        part = ref[:, :, pl.ds(start, HD)].astype(F32)
        return jnp.concatenate([part[r] for r in range(4)], axis=0)

    def attend(i, carry):
        g = i
        base = pl.multiple_of(g * HD, HD)
        keys_old = keys_v[:, :, pl.ds(base, HD)].reshape(128, HD)
        values_old = values_v[:, :, pl.ds(base, HD)].reshape(128, HD)
        keys_new = stacked(new_keys_v, base).astype(BF16)
        values_new = stacked(new_values_v, base).astype(BF16)
        query = jnp.concatenate(
            [stacked(queries_v, pl.multiple_of(g * 1024 + h * HD, HD)) for h in range(8)], axis=0
        ).astype(BF16)
        scaling = 1.0 / HD**0.5
        s_old = lax.dot_general(keys_old, query, NT, preferred_element_type=F32) * scaling
        s_new = lax.dot_general(keys_new, query, NT, preferred_element_type=F32) * scaling
        s_old = jnp.where(live_old, s_old, NEGATIVE)
        s_new = jnp.where(live_new, s_new, NEGATIVE)
        top = jnp.maximum(
            jnp.max(s_old, axis=0, keepdims=True), jnp.max(s_new, axis=0, keepdims=True)
        )
        top = top.astype(BF16).astype(F32)
        p_old = jnp.where(live_old, jnp.exp(s_old - top), 0.0)
        p_new = jnp.where(live_new, jnp.exp(s_new - top), 0.0)
        total = jnp.sum(p_old, axis=0, keepdims=True) + jnp.sum(p_new, axis=0, keepdims=True)
        mix = lax.dot_general(
            p_old.astype(BF16), values_old, TN, preferred_element_type=F32
        ) + lax.dot_general(p_new.astype(BF16), values_new, TN, preferred_element_type=F32)
        high = total.astype(BF16).astype(F32)
        tile = jnp.where(
            row_n == 0,
            top,
            jnp.where(row_n == 1, high, jnp.where(row_n == 2, total - high, 0.0)),
        ).astype(BF16)
        mix = mix.astype(BF16)
        for e in range(2):
            state_out[2 * g + e, 0:64, :] = mix[e * 64 : e * 64 + 64]
            state_out[2 * g + e, 64:80, :] = tile
        return carry

    lax.fori_loop(0, 8, attend, 0)
    pl.semaphore_wait(barrier, 30)

    def send_state(k, carry):
        dest = far_mp(k)
        rcopy(
            state_out.at[dest], state_in.at[mp], state_sem.at[0], state_sem.at[1], at_mp(dest)
        ).start()
        return carry

    lax.fori_loop(0, 15, send_state, 0)

    def am_copy(way, step):
        if way == 0:
            shard, target = (z - step + 9) % 8, (z + 1) % 8
        else:
            shard, target = (z + step - 1) % 8, (z + 7) % 8
        ref = amateur.at[c, shard]
        return rcopy(ref, ref, am_send.at[way, step], am_recv.at[way, step], at_z(target))

    def am_relay(shard, cc):
        ref = amateur.at[cc, shard]
        return rcopy(ref, ref, am_rsend.at[shard], am_rrecv.at[shard], sibling)

    def am_advance(step):
        am_copy(0, step).wait_recv()
        if step < 4:
            am_copy(1, step).wait_recv()
            am_copy(0, step + 1).start()
            if step < 3:
                am_copy(1, step + 1).start()
            am_relay((z + step) % 8, c).start()
        am_relay((z - step + 8) % 8, c).start()

    am_copy(0, 1).start()
    am_copy(1, 1).start()
    am_relay(z, c).start()
    state_in[mp] = state_out[mp]
    fifteen = pl.ds(0, 15)
    state_all = rcopy(
        state_out.at[fifteen], state_in.at[fifteen], state_sem.at[0], state_sem.at[1], sibling
    )
    state_all.wait_recv()

    tiles = [state_in[k, 64:80, :].astype(F32) for k in range(16)]
    top = tiles[0][0:1]
    for k in range(1, 16):
        top = jnp.maximum(top, tiles[k][0:1])
    total = jnp.zeros((1, 128), F32)
    weights = jnp.zeros((128, 128), F32)
    for k in range(16):
        scale = jnp.exp(tiles[k][0:1] - top)
        total = total + scale * (tiles[k][1:2] + tiles[k][2:3])
        weights = jnp.where(row_i == k, scale, weights)
    scale_t[...] = (weights / total).T
    own = scale_t[pl.ds(pl.multiple_of((mp % 2) * 64, 64), 64), :]
    mixed = jnp.zeros((64, HD), F32)
    for k in range(16):
        mixed = mixed + own[:, k : k + 1] * state_in[k, 0:64, :].astype(F32)

    block = dp * 2 + sec
    attended[block] = mixed.astype(BF16).reshape(4, 16, HD)

    def send_attended(k, carry):
        ref = attended.at[block]
        rcopy(ref, ref, attended_sem.at[0], attended_sem.at[1], at_n(far_n(k))).start()
        return carry

    lax.fori_loop(0, 15, send_attended, 0)
    loads[2].wait()
    loads[5].wait()
    fifteen_a = attended.at[fifteen]
    attended_all = rcopy(fifteen_a, fifteen_a, attended_sem.at[0], attended_sem.at[1], sibling)
    attended_all.wait_recv()
    partial = jnp.zeros((256, 512), F32)
    for h in range(4):
        partial = partial + jnp.dot(
            attended[:, h].reshape(256, HD),
            weight_v[h * HD : (h + 1) * HD, :],
            preferred_element_type=F32,
        )
    part_out[...] = partial.astype(BF16).reshape(16, 16, 512)

    def send_part(k, carry):
        dest = far_mp(k)
        rcopy(
            part_out.at[dest], part_in.at[mp], part_sem.at[0], part_sem.at[1], at_mp(dest)
        ).start()
        return carry

    lax.fori_loop(0, 15, send_part, 0)
    part_in[mp] = part_out[mp]
    am_advance(1)
    part_all = rcopy(
        part_in.at[fifteen], part_in.at[fifteen], part_sem.at[0], part_sem.at[1], sibling
    )
    part_all.wait_recv()
    hidden = resid_v[...].astype(F32)
    projected = part_in[0].astype(F32)
    for k in range(1, 16):
        projected = projected + part_in[k].astype(F32)
    full[c, 3, v, u] = (hidden + projected).astype(BF16)

    def one(slot, target):
        return rcopy(
            full.at[c, 3, v, u], full.at[c, slot, v, u], one_send, one_recv.at[slot], at_z(target)
        )

    def send_one(k, carry):
        slot = k + (k + 1) // 4 - k // 7
        one(slot, (z + 11 - slot) % 8).start()
        return carry

    lax.fori_loop(0, 7, send_one, 0)

    def two(half, k):
        ref = full.at[c, pl.ds(half * 2, 2), v, u]
        return rcopy(
            ref, ref, two_send.at[half], two_recv.at[half], at_uv((u + k) % 4, v)
        )

    def three(k, zz, vv):
        ref = full.at[c, zz, vv]
        return rcopy(
            ref, ref, three_send.at[zz], three_recv.at[k, zz], at_uv(u, (v + k) % 4)
        )

    def relay(zz, cc):
        ref = full.at[cc, zz]
        return rcopy(ref, ref, relay_send.at[zz], relay_recv.at[zz], sibling)

    for half in range(4):

        def wait_one(zz, carry):
            @pl.when(zz != 3)
            def _():
                one(zz, z).wait_recv()

            return carry

        lax.fori_loop(half * 2, half * 2 + 2, wait_one, 0)
        for k in range(1, 4):
            two(half, k).start()

    am_advance(2)

    def two_all(half):
        ref = full.at[c, pl.ds(half * 2, 2), v, pl.ds(0, 3)]
        return rcopy(ref, ref, two_send.at[half], two_recv.at[half], sibling)

    def send_three(zz, carry):
        for k in (2, 1, 3):
            three(k, zz, v).start()
        return carry

    for half in range(2):
        two_all(half).wait_recv()
        lax.fori_loop(half * 2, half * 2 + 2, send_three, 0)
    am_advance(3)

    loads[3].wait()
    acc_a[...] = jnp.zeros_like(acc_a)
    acc_e[...] = jnp.zeros_like(acc_e)
    square_a[...] = jnp.zeros_like(square_a)
    square_e[...] = jnp.zeros_like(square_e)

    def am_block(j, carry):
        k = (z + 5 + j) % 8
        am_relay(k, 1 - c).wait_recv()
        parts = []
        squares = square_a[...]
        for cc in range(2):
            wide = amateur[cc, k, 0:256, :].astype(F32)
            gain = amateur[cc, k, 256:272, :].astype(F32)[2:3]
            squares = squares + wide[:, 0:128] * wide[:, 0:128] + wide[:, 128:] * wide[:, 128:]
            parts.append((wide * gain).astype(BF16))
        square_a[...] = squares
        acc_a[...] += lax.dot_general(
            ha_v[:, pl.ds(pl.multiple_of(k * 512, 512), 512)],
            jnp.concatenate(parts, axis=1),
            NT,
            preferred_element_type=F32,
        )
        return carry

    lax.fori_loop(0, 7, am_block, 0)
    ones = jnp.ones((8, 128), F32)

    def chosen_here():
        return iota((512, 256), 0).astype(F32) == target_v[0:1, :]

    def inverse_norm(ref, width):
        sums = lax.dot_general(
            ones, ref[...], NT, preferred_element_type=F32, precision=lax.Precision.HIGHEST
        )
        return lax.rsqrt(sums[0:1] / width + EPSILON)

    row8 = iota((8, 128), 0)

    def pack(rows):
        tile = jnp.zeros((8, 128), F32)
        for k, row in enumerate(rows):
            tile = jnp.where(row8 == k, row, tile)
        return tile

    def halves(rows):
        return pack([row[:, h * 128 : h * 128 + 128] for row in rows for h in range(2)])

    def join(tiles):
        top = tiles[0]
        for tile in tiles[1:]:
            top = jnp.maximum(top, tile)
        top = top[0:2]
        total, pick = jnp.zeros((2, 128), F32), jnp.zeros((2, 128), F32)
        for tile in tiles:
            total = total + tile[2:4] * jnp.exp(tile[0:2] - top)
            pick = pick + tile[4:6]
        return top, total, pick

    def joined(tiles):
        return pack([part[h : h + 1] for part in join(tiles) for h in range(2)])

    fifteen_p = stats_p.at[0, fifteen]
    seven_z = stats_z.at[0, pl.ds(0, 7)]

    def pair(which):
        return rcopy(
            stats_s.at[which, 0],
            stats_s.at[which, 1],
            stats_send.at[which, 0],
            stats_recv.at[which, 0],
            sibling,
        )

    def start_pair(which, rows):
        stats_s[which, 0] = halves(rows)
        pair(which).start()

    def start_p(which):
        pair(which).wait_recv()
        stats_p[which, mp] = joined([stats_s[which, 0], stats_s[which, 1]])

        def send_p(k, carry):
            ref = stats_p.at[which, mp]
            rcopy(
                ref, ref, stats_send.at[which, 1], stats_recv.at[which, 1], at_mp(far_mp(k))
            ).start()
            return carry

        lax.fori_loop(0, 15, send_p, 0)

    def p_all(which):
        return rcopy(
            fifteen_p, fifteen_p, stats_send.at[which, 1], stats_recv.at[which, 1], sibling
        )

    def start_z(which):
        p_all(which).wait_recv()
        stats_z[which, z] = joined([stats_p[which, k] for k in range(16)])

        def send_z(k, carry):
            ref = stats_z.at[which, z]
            rcopy(
                ref, ref, stats_send.at[which, 2], stats_recv.at[which, 2], at_z((z + hop(k)) % 8)
            ).start()
            return carry

        lax.fori_loop(0, 7, send_z, 0)

    def z_all(which):
        return rcopy(seven_z, seven_z, stats_send.at[which, 2], stats_recv.at[which, 2], sibling)

    def settle(which):
        pair(which).wait_send()
        p_all(which).wait_send()
        z_all(which).wait_send()

    two_all(2).wait_recv()
    two_all(3).wait_recv()
    loads[4].wait()

    def gather_block(zz, carry):
        @pl.when(zz < 8)
        def _():
            for k in (1, 3, 2):
                three(k, zz, (v - k + 4) % 4).wait_recv()
            relay(zz, c).start()

            @pl.when(zz < 4)
            def _():
                send_three(zz + 4, 0)


        @pl.when(zz >= 1)
        def _():
            k = zz - 1
            relay(k, 1 - c).wait_recv()
            parts = []
            squares = square_e[...]
            for cc in range(2):
                wide = full[cc, k]
                if cc == 0:
                    wide = jnp.swapaxes(wide, 0, 1)
                wide = wide.reshape(256, 512).astype(F32)
                tile = amateur[cc, (z + 5 + k) % 8, 256:272, :].astype(F32)
                for half in range(2):
                    piece = wide[:, half * 256 : half * 256 + 256]
                    squares = (
                        squares
                        + piece[:, 0:128] * piece[:, 0:128]
                        + piece[:, 128:] * piece[:, 128:]
                    )
                    parts.append((piece * tile[half : half + 1]).astype(BF16))
            square_e[...] = squares
            acc_e[...] += lax.dot_general(
                he_v[:, pl.ds(pl.multiple_of((z + 5 + k) % 8 * 1024, 1024), 1024)],
                jnp.concatenate(parts, axis=1),
                NT,
                preferred_element_type=F32,
            )

        return carry

    lax.fori_loop(0, 3, gather_block, 0)
    am_advance(4)
    lax.fori_loop(3, 4, gather_block, 0)
    lax.fori_loop(7, 8, am_block, 0)
    logits_a = acc_a[...] * inverse_norm(square_a, 4096.0)
    acc_a[...] = logits_a
    top_a = jnp.max(logits_a, axis=0, keepdims=True)
    total_a = jnp.sum(jnp.exp(logits_a - top_a), axis=0, keepdims=True)
    picked_a = jnp.sum(jnp.where(chosen_here(), logits_a, 0.0), axis=0, keepdims=True)
    start_pair(1, (top_a, total_a, picked_a))
    lax.fori_loop(4, 6, gather_block, 0)
    start_p(1)
    lax.fori_loop(6, 9, gather_block, 0)

    logits_e = acc_e[...] * inverse_norm(square_e, 8192.0)
    top_e = jnp.max(logits_e, axis=0, keepdims=True)
    total_e = jnp.sum(jnp.exp(logits_e - top_e), axis=0, keepdims=True)
    picked = jnp.sum(jnp.where(chosen_here(), logits_e, 0.0), axis=0, keepdims=True)

    start_pair(0, (top_e, total_e, picked))
    start_p(0)
    start_z(1)
    diff[...] = (logits_e - CONTRAST * acc_a[...]).T
    store = pltpu.make_async_copy(diff, out_diff, load_sem.at[10])
    store.start()

    state_all.wait_send()
    attended_all.wait_send()
    for step in range(1, 5):
        am_copy(0, step).wait_send()
        if step < 4:
            am_copy(1, step).wait_send()
    part_all.wait_send()
    ref = full.at[c, pl.ds(0, 7), v, u]
    rcopy(ref, ref, one_send, one_recv.at[0], sibling).wait_send()
    for half in range(4):
        two_all(half).wait_send()

    def drain(k, carry):
        relay(k, c).wait_send()
        am_relay(k, c).wait_send()
        ref = full.at[c, k, pl.ds(0, 3)]
        rcopy(ref, ref, three_send.at[k], three_recv.at[1, k], sibling).wait_send()
        return carry

    lax.fori_loop(0, 8, drain, 0)
    start_z(0)
    settle(1)
    z_all(1).wait_recv()
    top, total, pick_a = join([stats_z[1, k] for k in range(8)])
    lse_a = top + jnp.log(total)
    z_all(0).wait_recv()
    top, total, pick = join([stats_z[0, k] for k in range(8)])
    shift = top + jnp.log(total) - CONTRAST * lse_a
    chosen_row = pick - CONTRAST * pick_a - shift
    shift = jnp.concatenate([shift[0:1], shift[1:2]], axis=1)
    chosen_row = jnp.concatenate([chosen_row[0:1], chosen_row[1:2]], axis=1)
    row_8 = iota((8, 256), 0)
    out_rows[...] = jnp.where(row_8 == 0, shift, jnp.where(row_8 == 1, chosen_row, 0.0))
    store.wait()
    settle(0)


def finish(diff, rows, out, out_chosen):
    shift = jnp.broadcast_to(rows[0:1, :], (128, 256)).T
    out[...] = (diff[...] - shift[:, 0:1]).reshape(64, 4, 512).astype(BF16)
    pick_row = (iota((64, 256), 1) // 4 == iota((64, 256), 0)).astype(F32)
    step_row = iota((8, 256), 1) % 4 == iota((8, 256), 0)
    masked = jnp.where(step_row, rows[1:2, :], 0.0)
    out_chosen[...] = lax.dot_general(
        masked, pick_row, NT, preferred_element_type=F32, precision=lax.Precision.HIGHEST
    )[0:4]


def local(
    queries,
    new_keys,
    new_values,
    cache_keys,
    cache_values,
    lengths,
    out_weight,
    resid_expert,
    gain_expert,
    hidden_amateur,
    gain_amateur,
    head_expert,
    head_amateur,
    chosen,
):
    vmem = pl.BlockSpec(memory_space=pltpu.VMEM)
    hbm = pl.BlockSpec(memory_space=pl.ANY)
    dma = pltpu.SemaphoreType.DMA
    diff, rows = pl.pallas_call(
        kernel,
        out_shape=(
            jax.ShapeDtypeStruct((256, 512), F32),
            jax.ShapeDtypeStruct((8, 256), F32),
        ),
        in_specs=[pl.BlockSpec(memory_space=pltpu.SMEM)]
        + [hbm] * 4
        + [vmem] * 2
        + [hbm]
        + [vmem]
        + [hbm] * 5,
        out_specs=(hbm, vmem),
        scratch_shapes=[
            pltpu.VMEM((4, 4, 8192), BF16),
            pltpu.VMEM((4, 4, 1024), BF16),
            pltpu.VMEM((4, 4, 1024), BF16),
            pltpu.VMEM((16, 512), BF16),
            pltpu.VMEM((4, 32, 1024), BF16),
            pltpu.VMEM((4, 32, 1024), BF16),
            pltpu.VMEM((512, 512), BF16),
            pltpu.VMEM((512, 8192), BF16),
            pltpu.VMEM((512, 4096), BF16),
            pltpu.VMEM((16, 80, 128), BF16),
            pltpu.VMEM((16, 80, 128), BF16),
            pltpu.VMEM((128, 128), F32),
            pltpu.VMEM((16, 4, 16, 128), BF16),
            pltpu.VMEM((16, 16, 512), BF16),
            pltpu.VMEM((16, 16, 512), BF16),
            pltpu.VMEM((2, 8, 4, 4, 16, 512), BF16),
            pltpu.VMEM((2, 8, 272, 256), BF16),
            pltpu.VMEM((512, 256), F32),
            pltpu.VMEM((512, 256), F32),
            pltpu.VMEM((256, 128), F32),
            pltpu.VMEM((256, 128), F32),
            pltpu.VMEM((256, 512), F32),
            pltpu.VMEM((8, 256), F32),
            pltpu.VMEM((2, 2, 8, 128), F32),
            pltpu.VMEM((2, 16, 8, 128), F32),
            pltpu.VMEM((2, 8, 8, 128), F32),
            dma((11,)),
            dma((2,)),
            dma((2,)),
            dma((2,)),
            dma,
            dma((8,)),
            dma((4,)),
            dma((4,)),
            dma((8,)),
            dma((4, 8)),
            dma((8,)),
            dma((8,)),
            dma((2, 5)),
            dma((2, 5)),
            dma((8,)),
            dma((8,)),
            dma((2, 3)),
            dma((2, 3)),
        ],
        compiler_params=pltpu.CompilerParams(
            collective_id=0, has_side_effects=True, vmem_limit_bytes=56 * 1024 * 1024
        ),
        name="contrast",
    )(
        lengths,
        queries,
        new_keys,
        new_values,
        resid_expert,
        gain_expert,
        gain_amateur,
        hidden_amateur,
        chosen.T,
        cache_keys,
        cache_values,
        out_weight,
        head_expert,
        head_amateur,
    )
    scores, chosen_score = pl.pallas_call(
        finish,
        out_shape=(
            jax.ShapeDtypeStruct((64, 4, 512), BF16),
            jax.ShapeDtypeStruct((4, 64), F32),
        ),
        in_specs=[vmem] * 2,
        out_specs=(vmem, vmem),
        name="finish",
    )(diff, rows)
    return scores, chosen_score.T


def solution(mesh):
    return jax.shard_map(
        local,
        mesh=mesh,
        in_specs=(
            P("dp", None, None),
            P("dp", None, None),
            P("dp", None, None),
            P("dp", "mp", None),
            P("dp", "mp", None),
            P("dp"),
            P("mp", ("section", "dp")),
            P(None, ("section", "dp")),
            P(("section", "dp")),
            P(None, ("section", "dp")),
            P(("section", "dp")),
            P(("section", "dp", "mp"), None),
            P(("section", "dp", "mp"), None),
            P(),
        ),
        out_specs=(P(None, None, ("section", "dp", "mp")), P()),
        check_vma=False,
    )
```
